256 devices in a mesh: gx: 16 (over x, z_hi), gy: 4 (over y), gz: 4 (over z_lo, core).
Axes of the slice: x: 4, y: 4, z: 8 (z_hi: 4, z_lo: 2; z = z_hi * 2 + z_lo), core: 2. Of those that a mesh axis runs over, the one named last changes fastest.
Arguments:
- right_side: float32 [256, 64, 1024], P('gx', 'gy', 'gz'), may hold values from -5 to 5
- coefficients: float32 [4, 256, 64, 1024], P(None, 'gx', 'gy', 'gz'), may hold values from 0.1 to 32
- first_guess: float32 [256, 64, 1024], P('gx', 'gy', 'gz'), may hold values from -3 to 3
Outputs:
- solution_field: float32 [256, 64, 1024], P('gx', 'gy', 'gz')
The draws below stay inside these ranges and needn't reach their ends.
All inputs are finite; a program needn't handle non-finite values.
Results may differ from the reference program's by a relative error of at most 0.00002.
Values sent between devices are 32-bit elements; how exact they have to be, the bound alone decides.
No kernel may reach another device: no remote copies, remote signals or barrier semaphores. Data moves between devices by JAX's collectives and lax.ppermute only.
A program may use at most 128 MiB of HBM per device.

```python
import jax
import jax.numpy as jnp
from jax import lax

CYCLES = 2
SWEEPS = 8
NX = 256
NY = 64
NZ = 1024


slab_width = 64


def draw_coefficients(key, part):
    first_pos = jnp.arange(NX, dtype=jnp.int32)[:, None, None]
    second_pos = jnp.arange(NY, dtype=jnp.int32)[None, :, None]
    third_pos = jnp.arange(NZ, dtype=jnp.int32)[None, None, :]
    slab_number = (first_pos + second_pos + third_pos) // slab_width % 3
    members = jnp.arange(3, dtype=jnp.int32)[:, None, None, None]
    strong = slab_number[None] == members
    diffusion_low = jnp.where(strong, jnp.float32(16.0), jnp.float32(0.15))
    diffusion_high = jnp.where(strong, jnp.float32(32.0), jnp.float32(0.3))
    reaction_low = jnp.full((1, NX, NY, NZ), 0.1, jnp.float32)
    reaction_high = jnp.full((1, NX, NY, NZ), 1.0, jnp.float32)
    lowest = jnp.concatenate([diffusion_low, reaction_low], 0)
    highest = jnp.concatenate([diffusion_high, reaction_high], 0)
    uniform_draw = jax.random.uniform(jax.random.fold_in(key, 11), (4, NX, NY, NZ), jnp.float32)
    return lowest * jnp.exp(uniform_draw * jnp.log(highest / lowest))


def draw_right_side(key, part):
    noise = jax.random.normal(jax.random.fold_in(key, 23), (NX, NY, NZ), jnp.float32)
    return jnp.clip(noise, -5.0, 5.0)


def steps_of(key, extent, shards, low, top_value):
    factor_of, own = 1.0, jax.random.fold_in(key, 6)
    for position, shards_of in shards:
        draws = jnp.exp(jax.random.uniform(jax.random.fold_in(own, position), (shards_of,), jnp.float32, low / len(shards), top_value / len(shards)))
        factor_of = factor_of * jnp.repeat(draws, extent[position] // shards_of).reshape([-1 if axis == position else 1 for axis in range(len(extent))])
    return factor_of


def scatter_about(stream_key, dims, width, reach, pieces=(), held_as=jnp.bfloat16):
    values = jax.random.normal(stream_key, dims, jnp.float32) * width
    if len(pieces) > 0:
        values = steps_of(stream_key, dims, pieces, -0.22, 0.18) * values
    return jnp.clip(values, min=-reach, max=reach).astype(held_as)


def setup_inputs(seed: int = 0) -> dict:
    streams_of = jax.random.split(jax.random.key(seed), 4)
    right_side = draw_right_side(jax.random.fold_in(streams_of[3], 71), 0)
    coefficients = draw_coefficients(jax.random.fold_in(streams_of[3], 71), 0)
    first_guess = scatter_about(streams_of[2], (NX, NY, NZ), 0.5, 3.0, ((0, 16), (1, 4), (2, 4)), jnp.float32)
    return {"right_side": right_side, "coefficients": coefficients, "first_guess": first_guess}


relaxation = 0.8
blending = 0.4


def pad_along(values, direction):
    widths = [(0, 0)] * values.ndim
    widths[direction] = (1, 1)
    return jnp.pad(values, widths)


def neighbours(values, direction):
    length = values.shape[direction]
    padded = pad_along(values, direction)
    upper_cells = lax.slice_in_dim(padded, 2, length + 2, axis=direction)
    lower_cells = lax.slice_in_dim(padded, 0, length, axis=direction)
    return upper_cells, lower_cells


def face_weights(fields):
    diagonal = fields[3]
    weights = []
    for direction in range(3):
        upper_cells, lower_cells = neighbours(fields[direction], direction)
        weight_high = 0.5 * (fields[direction] + upper_cells)
        weight_low = 0.5 * (fields[direction] + lower_cells)
        weights.append((weight_high, weight_low))
        diagonal = diagonal + weight_high + weight_low
    return weights, diagonal


def operate(values, reaction, weights):
    result = reaction * values
    for direction in range(3):
        weight_high, weight_low = weights[direction]
        upper_cells, lower_cells = neighbours(values, direction)
        result = result + (weight_high * (values - upper_cells) + weight_low * (values - lower_cells))
    return result


def pair_mean(values, direction):
    shape = values.shape
    split_shape = shape[:direction] + (shape[direction] // 2, 2) + shape[direction + 1:]
    paired = values.reshape(split_shape)
    even_cells = lax.index_in_dim(paired, 0, direction + 1, keepdims=False)
    odd_cells = lax.index_in_dim(paired, 1, direction + 1, keepdims=False)
    return 0.5 * (even_cells + odd_cells)


def coarse_fields(fields, direction):
    averaged = pair_mean(fields, direction + 1)
    factors = [1.0, 1.0, 1.0, 1.0]
    factors[direction] = 0.25
    return jnp.stack([averaged[member] * factors[member] for member in range(4)])


def prolong_padded(padded, direction):
    length = padded.shape[direction] - 2
    middle = lax.slice_in_dim(padded, 1, length + 1, axis=direction)
    upper_cells = lax.slice_in_dim(padded, 2, length + 2, axis=direction)
    lower_cells = lax.slice_in_dim(padded, 0, length, axis=direction)
    even_cells = 0.75 * middle + 0.25 * lower_cells
    odd_cells = 0.75 * middle + 0.25 * upper_cells
    joined = jnp.stack([even_cells, odd_cells], direction + 1)
    new_shape = list(middle.shape)
    new_shape[direction] = 2 * length
    return joined.reshape(new_shape)


def reference(right_side, coefficients, first_guess):
    weights, diagonal = face_weights(coefficients)
    branches = []
    for direction in range(3):
        coarse = coarse_fields(coefficients, direction)
        coarse_weights, coarse_diagonal = face_weights(coarse)
        branches.append((coarse[3], coarse_weights, coarse_diagonal))
    solution_field = first_guess
    for cycle_index in range(CYCLES):
        residual = right_side - operate(solution_field, coefficients[3], weights)
        update = None
        for direction in range(3):
            coarse_reaction, coarse_weights, coarse_diagonal = branches[direction]
            coarse_residual = pair_mean(residual, direction)
            errors = jnp.zeros_like(coarse_residual)
            for repeat in range(SWEEPS):
                errors = errors + relaxation * (coarse_residual - operate(errors, coarse_reaction, coarse_weights)) / coarse_diagonal
            correction = prolong_padded(pad_along(errors, direction), direction)
            update = correction if update is None else update + correction
        solution_field = solution_field + blending * update
    return solution_field
```

```python
import functools

import jax
import jax.numpy as jnp
from jax import lax
from jax.experimental import pallas as pl
from jax.experimental.pallas import tpu as pltpu
from jax.sharding import PartitionSpec as P

CYCLES = 2
SWEEPS = 8
relaxation = 0.8
blending = 0.4

PLANES = (8, 16, 16)
HALO = (8, 7, 7)
WIDE = (24, 30, 30)
ROWT = (2, 1, 2)
LANET = (2, 2, 1)
S_AT = (0, 32, 64)
X_AT = (0, 32, 46)
Y_AT = (0, 48, 108)
Z_AT = (0, 96, 192)
NS, NXT, NYT, NZG = 96, 60, 138, 20
EXT = tuple((WIDE[b], 8 * (ROWT[b] + 2), 128 * (LANET[b] + 1)) for b in range(3))
F32 = jnp.float32
VMEM_LIMIT = 60 * 1024 * 1024
HIGHEST = lax.Precision.HIGHEST


def lane_of(shape):
    return lax.broadcasted_iota(jnp.int32, shape, len(shape) - 1)


def row_of(shape):
    return lax.broadcasted_iota(jnp.int32, shape, len(shape) - 2)


def pack_rows(load):
    groups = []
    for g in range(4):
        acc = jnp.zeros((8, 256), F32)
        for j in range(4):
            value, turn = load(4 * g + j)
            turn = (turn + 2 * j) % 8
            value = pltpu.roll(value, turn, 0) if turn else value
            acc = jnp.where(row_of((8, 256)) // 2 == j, value, acc)
        groups.append(acc)
    return groups


def pack_lanes(load):
    acc = jnp.zeros((16, 128), F32)
    for j in range(16):
        value, turn = load(j)
        turn = (turn + 8 * j) % 128
        value = pltpu.roll(value, turn, 1) if turn else value
        acc = jnp.where(lane_of((16, 128)) // 8 == j, value, acc)
    return acc


def send_faces(at, row_field, lane_field, yl, yh, zl, zh):
    for g, value in enumerate(pack_rows(lambda x: (row_field(x)[0:8, :], 0))):
        yl[at, g] = value
    for g, value in enumerate(pack_rows(lambda x: (row_field(x)[8:16, :], 2))):
        yh[at, g] = value
    zl[at] = pack_lanes(lambda x: (lane_field(x)[:, 0:128], 0))
    zh[at] = pack_lanes(lambda x: (lane_field(x)[:, 128:256], 8))


def faces_kernel(k, u, xl, xh, yl, yh, zl, zh):
    xl[0:1] = u[0:1]
    xl[1:3] = k[0, 0:2]
    xh[0:1] = u[15:16]
    xh[1:3] = k[0, 14:16]
    send_faces(0, lambda x: u[x], lambda x: u[x], yl, yh, zl, zh)
    send_faces(1, lambda x: k[1, x], lambda x: k[2, x], yl, yh, zl, zh)


def halo_rows(value, at, yl, yh, m):
    high, low = [], []
    for x in range(16):
        g, j = divmod(x, 4)
        high.append(pltpu.roll(yh[at, g], (8 - 2 * j) % 8, 0) if j else yh[at, g])
        turn = (6 - 2 * j) % 8
        low.append(pltpu.roll(yl[at, g], turn, 0) if turn else yl[at, g])
    high = jnp.stack(high) * m[3]
    low = jnp.stack(low) * m[2]
    return jnp.concatenate([value, high, low], axis=1)


def halo_lanes(value, at, zl, zh, m):
    high = zh[at] * m[5]
    low = zl[at] * m[4]
    lane = lane_of((16, 128))
    tiles = []
    for x in range(16):
        a = pltpu.roll(high, (128 - 8 * x) % 128, 1) if x else high
        b = pltpu.roll(low, 120 - 8 * x, 1) if x < 15 else low
        tiles.append(jnp.where(lane < 8, a, jnp.where(lane >= 120, b, 0.0)))
    return jnp.concatenate([value, jnp.stack(tiles)], axis=2)


def up(value, axis, keep):
    return keep(pltpu.roll(value, value.shape[axis] - 1, axis))


def down(value, axis, keep):
    return keep(pltpu.roll(value, 1, axis))


def lane_means(value, lanes):
    planes, rows, width = value.shape
    source = lax.broadcasted_iota(jnp.int32, (width, lanes), 0)
    target = lax.broadcasted_iota(jnp.int32, (width, lanes), 1)
    pair = source // 2
    pair = jnp.where(source >= 320, pair + 64, pair)
    matrix = jnp.where(pair == target, jnp.float32(0.5), jnp.float32(0.0))
    out = jnp.dot(value.reshape(planes * rows, width), matrix, precision=HIGHEST, preferred_element_type=F32)
    return out.reshape(planes, rows, lanes)


def row_means(value, scratch):
    planes, rows, width = value.shape
    count = planes * rows
    parts = []
    for t in range(width // 128):
        scratch[t, 0:count] = value[:, :, 128 * t : 128 * t + 128].reshape(count, 128)
        even = scratch[t, pl.ds(0, count // 2, stride=2), :]
        odd = scratch[t, pl.ds(1, count // 2, stride=2), :]
        parts.append((0.5 * (even + odd)).reshape(planes, rows // 2, 128))
    return jnp.concatenate(parts, axis=2)


def plane_means(value):
    planes = value.shape[0]
    value = value.reshape((planes // 2, 2) + value.shape[1:])
    return 0.5 * (value[:, 0] + value[:, 1])


def residual_of(k, u, f, kfaces, ufaces, m):
    xl, xh, yl, yh, zl, zh = kfaces
    uxl, uxh, uyl, uyh, uzl, uzh = ufaces
    own, rows, lanes = (lambda v: v), (lambda v: v[:, 0:16]), (lambda v: v[:, :, 0:256])
    v = u[...]
    k0 = k[0]
    vx = jnp.concatenate([uxl[0:1] * m[0], v, uxh[0:1] * m[1]], axis=0)
    kx = jnp.concatenate([xl[2:3] * m[0], k0, xh[1:2] * m[1]], axis=0)
    total = k[3] * v
    total = total + 0.5 * (k0 + kx[2:18]) * (v - vx[2:18]) + 0.5 * (k0 + kx[0:16]) * (v - vx[0:16])
    vy = halo_rows(v, 0, uyl, uyh, m)
    k1 = k[1]
    ky = halo_rows(k1, 1, yl, yh, m)
    total = total + 0.5 * (k1 + up(ky, 1, rows)) * (v - up(vy, 1, rows))
    total = total + 0.5 * (k1 + down(ky, 1, rows)) * (v - down(vy, 1, rows))
    vz = halo_lanes(v, 0, uzl, uzh, m)
    k2 = k[2]
    kz = halo_lanes(k2, 1, zl, zh, m)
    total = total + 0.5 * (k2 + up(kz, 2, lanes)) * (v - up(vz, 2, lanes))
    total = total + 0.5 * (k2 + down(kz, 2, lanes)) * (v - down(vz, 2, lanes))
    return f[...] - total, ky, kz


def put(out, field, b, value):
    for yt in range(ROWT[b]):
        for lt in range(LANET[b]):
            at = S_AT[b] + (yt * LANET[b] + lt) * PLANES[b]
            out[field, at : at + PLANES[b]] = value[:, 8 * yt : 8 * yt + 8, 128 * lt : 128 * lt + 128]


def put_sides(out, field, b, xlo, xhi):
    h, p = HALO[b], PLANES[b]
    for t in range(ROWT[b] * LANET[b]):
        to, at = X_AT[b] + t * h, S_AT[b] + t * p
        xlo[field, to : to + h] = out[field, at : at + h]
        xhi[field, to : to + h] = out[field, at + p - h : at + p]


def coarse_residuals(r, scratch):
    return plane_means(r), row_means(r, scratch), lane_means(r, 128)


def fields_kernel(m, k, u, f, xl, xh, yl, yh, zl, zh, out, xlo, xhi, scratch):
    faces = (xl, xh, yl, yh, zl, zh)
    r, ky, kz = residual_of(k, u, f, faces, faces, m)
    kx = jnp.concatenate([xl[1:3] * m[0], k[0], xh[1:3] * m[1]], axis=0)
    coarse = [
        (plane_means(kx), plane_means(ky), plane_means(kz), plane_means(k[3])),
        (row_means(kx[1:19], scratch), row_means(ky, scratch), row_means(kz, scratch), row_means(k[3], scratch)),
        (lane_means(kx[1:19], 128), lane_means(ky, 128), lane_means(kz, 256), lane_means(k[3], 128)),
    ]
    residuals = coarse_residuals(r, scratch)
    for b in range(3):
        cx, cy, cz, s = coarse[b]
        p, nr, nl = PLANES[b], 8 * ROWT[b], 128 * LANET[b]
        scale = [0.5, 0.5, 0.5]
        scale[b] = 0.125
        rows, lanes = (lambda v: v[:, 0:nr]), (lambda v: v[:, :, 0:nl])
        w0l = scale[0] * (cx[1 : p + 1] + cx[0:p])
        w0h = scale[0] * (cx[1 : p + 1] + cx[2 : p + 2])
        w1l = scale[1] * (rows(cy) + down(cy, 1, rows))
        w1h = scale[1] * (rows(cy) + up(cy, 1, rows))
        w2l = scale[2] * (lanes(cz) + down(cz, 2, lanes))
        w2h = scale[2] * (lanes(cz) + up(cz, 2, lanes))
        c = relaxation / (s + w0l + w0h + w1l + w1h + w2l + w2h)
        for field, value in enumerate((c * residuals[b], c, w0l, w1l, w2l)):
            put(out, field, b, value)
            put_sides(out, field, b, xlo, xhi)


def residual_kernel(m, k, u, f, c, xl, xh, yl, yh, zl, zh, uxl, uxh, uyl, uyh, uzl, uzh, out, xlo, xhi, scratch):
    r, _, _ = residual_of(k, u, f, (xl, xh, yl, yh, zl, zh), (uxl, uxh, uyl, uyh, uzl, uzh), m)
    for b, value in enumerate(coarse_residuals(r, scratch)):
        put(out, 0, b, value)
    out[0] = out[0] * c[1]
    for b in range(3):
        put_sides(out, 0, b, xlo, xhi)


def own_pieces(field, b, yt, lt, m, s, xl, xh):
    h, p = HALO[b], PLANES[b]
    t = yt * LANET[b] + lt
    at, own = X_AT[b] + t * h, S_AT[b] + t * p
    yield 0, h, xl[field, at : at + h] * m[0]
    yield h, p, s[field, own : own + p]
    yield h + p, h, xh[field, at : at + h] * m[1]


def pieces(field, b, yt, lt, m, s, xl, xh, yl, yh):
    if yt < ROWT[b]:
        yield from own_pieces(field, b, yt, lt, m, s, xl, xh)
        return
    at = Y_AT[b] + lt * WIDE[b]
    source, mask = (yh, m[3]) if yt == ROWT[b] else (yl, m[2])
    yield 0, WIDE[b], source[field, at : at + WIDE[b]] * mask


def rows_kernel(fields, m, s, xl, xh, ylo, yhi):
    for field in range(fields):
        for b in range(3):
            for lt in range(LANET[b]):
                at = Y_AT[b] + lt * WIDE[b]
                for x, n, value in own_pieces(field, b, 0, lt, m, s, xl, xh):
                    ylo[field, at + x : at + x + n] = value
                for x, n, value in own_pieces(field, b, ROWT[b] - 1, lt, m, s, xl, xh):
                    yhi[field, at + x : at + x + n] = value


def lanes_kernel(fields, m, s, xl, xh, yl, yh, zlo, zhi, low, high):
    lane = lane_of((NZG, 8, 128))
    for start in (186, 312):
        stop = 192 if start == 186 else 320
        low[start:stop] = jnp.zeros((stop - start, 8, 128), F32)
        high[start:stop] = jnp.zeros((stop - start, 8, 128), F32)
    for field in range(fields):
        for b in range(3):
            for yt in range(ROWT[b] + 2):
                at = Z_AT[b] + yt * WIDE[b]
                for x, n, value in pieces(field, b, yt, 0, m, s, xl, xh, yl, yh):
                    low[at + x : at + x + n] = value
                for x, n, value in pieces(field, b, yt, LANET[b] - 1, m, s, xl, xh, yl, yh):
                    high[at + x : at + x + n] = value
        a = jnp.zeros((NZG, 8, 128), F32)
        z = jnp.zeros((NZG, 8, 128), F32)
        for j in range(16):
            v = low[NZG * j : NZG * j + NZG]
            a = jnp.where(lane // 8 == j, pltpu.roll(v, 8 * j, 2) if j else v, a)
            v = high[NZG * j : NZG * j + NZG]
            z = jnp.where(lane // 8 == j, pltpu.roll(v, 8 * j + 8, 2) if j < 15 else v, z)
        zlo[field] = a
        zhi[field] = z


def assemble(field, m, s, xl, xh, yl, yh, zl, zh, halo, ext):
    lane = lane_of((NZG, 8, 128))
    high = zh[field] * m[5]
    low = zl[field] * m[4]
    for j in range(16):
        a = pltpu.roll(high, 128 - 8 * j, 2) if j else high
        b = pltpu.roll(low, 120 - 8 * j, 2) if j < 15 else low
        halo[NZG * j : NZG * j + NZG] = jnp.where(lane < 8, a, jnp.where(lane >= 120, b, 0.0))
    for b in range(3):
        for yt in range(ROWT[b] + 2):
            for lt in range(LANET[b]):
                for x, n, value in pieces(field, b, yt, lt, m, s, xl, xh, yl, yh):
                    ext[b][field, x : x + n, 8 * yt : 8 * yt + 8, 128 * lt : 128 * lt + 128] = value
            at = Z_AT[b] + yt * WIDE[b]
            tile = 128 * LANET[b]
            ext[b][field, :, 8 * yt : 8 * yt + 8, tile : tile + 128] = halo[at : at + WIDE[b]]


def scaled_weights(b, ext, weights):
    wide, rows, lanes = EXT[b]

    def plane(x, carry):
        c, w0, w1, w2 = (ext[field, x] for field in range(1, 5))
        weights[0, x] = c * w0
        weights[1, x] = c * ext[2, x + 1]
        weights[2, x] = c * w1
        weights[3, x] = c * pltpu.roll(w1, rows - 1, 0)
        weights[4, x] = c * w2
        weights[5, x] = c * pltpu.roll(w2, lanes - 1, 1)
        return carry

    lax.fori_loop(1, wide - 1, plane, 0)


def sweeps(b, ext, weights):
    wide, rows, lanes = EXT[b]
    source = 0
    for sweep in range(1, SWEEPS):
        target = 1 if source != 1 else 2

        def plane(x, carry, source=source, target=target):
            e = ext[source, x]
            total = ext[0, x] + (1.0 - relaxation) * e
            total = total + (weights[0, x] * ext[source, x - 1] + weights[1, x] * ext[source, x + 1])
            total = total + (weights[2, x] * pltpu.roll(e, 1, 0) + weights[3, x] * pltpu.roll(e, rows - 1, 0))
            total = total + (weights[4, x] * pltpu.roll(e, 1, 1) + weights[5, x] * pltpu.roll(e, lanes - 1, 1))
            ext[target, x] = total
            return carry

        lax.fori_loop(sweep, wide - sweep, plane, 0)
        source = target
    return source


def cycle_kernel(first, *refs):
    m, u, s, xl, xh, yl, yh, zl, zh = refs[:9]
    if first:
        unew, w0, w1, w2, uxlo, uxhi, uylo, uyhi, uzlo, uzhi = refs[9:19]
        rest = refs[19:]
    else:
        w0, w1, w2, unew = refs[9:13]
        rest = refs[13:]
    halo, joined, e0, e1, e2 = rest
    ext, weights = (e0, e1, e2), (w0, w1, w2)
    for field in range(5 if first else 1):
        assemble(field, m, s, xl, xh, yl, yh, zl, zh, halo, ext)
    last = []
    for b in range(3):
        if first:
            scaled_weights(b, ext[b], weights[b])
        last.append(sweeps(b, ext[b], weights[b]))
    for x in range(16):
        e = e1[last[1], 7 + x]
        even = 0.75 * e + 0.25 * pltpu.roll(e, 1, 0)
        odd = 0.75 * e + 0.25 * pltpu.roll(e, 23, 0)
        for t in range(2):
            joined[t, pl.ds(16 * x, 8, stride=2), :] = even[0:8, 128 * t : 128 * t + 128]
            joined[t, pl.ds(16 * x + 1, 8, stride=2), :] = odd[0:8, 128 * t : 128 * t + 128]
    source = lax.broadcasted_iota(jnp.int32, (256, 256), 0)
    target = lax.broadcasted_iota(jnp.int32, (256, 256), 1)
    near = target // 2
    far = (near + 2 * (target % 2) - 1 + 256) % 256
    matrix = jnp.where(source == near, 0.75, jnp.where(source == far, 0.25, 0.0)).astype(F32)
    along = jnp.dot(
        e2[last[2], 7:23, 0:16, :].reshape(256, 256), matrix, precision=HIGHEST, preferred_element_type=F32
    ).reshape(16, 16, 256)
    for x in range(16):
        i = 8 + x // 2
        other = i + 1 if x % 2 else i - 1
        first_part = 0.75 * e0[last[0], i, 0:16, 0:256] + 0.25 * e0[last[0], other, 0:16, 0:256]
        second = jnp.concatenate([joined[0, 16 * x : 16 * x + 16], joined[1, 16 * x : 16 * x + 16]], axis=1)
        unew[x] = u[x] + blending * ((first_part + second) + along[x])
    if first:
        uxlo[0:1] = unew[0:1]
        uxhi[0:1] = unew[15:16]
        send_faces(0, lambda x: unew[x], lambda x: unew[x], uylo, uyhi, uzlo, uzhi)


def ring(value, axis, step):
    n = lax.axis_size(axis)
    return lax.ppermute(value, axis, [(i, (i + step) % n) for i in range(n)])


def both(axis, to_low, to_high):
    return ring(to_high, axis, 1), ring(to_low, axis, -1)


def call(kernel, outs, args, scratch=(), masked=True):
    vmem = pl.BlockSpec(memory_space=pltpu.VMEM)
    specs = [vmem] * len(args)
    if masked:
        specs[0] = pl.BlockSpec(memory_space=pltpu.SMEM)
    return pl.pallas_call(
        kernel,
        out_shape=[jax.ShapeDtypeStruct(shape, F32) for shape in outs],
        in_specs=specs,
        out_specs=[vmem] * len(outs),
        scratch_shapes=[pltpu.VMEM(shape, F32) for shape in scratch],
        compiler_params=pltpu.CompilerParams(vmem_limit_bytes=VMEM_LIMIT),
    )(*args)


def face_shapes(fields):
    return [(2 * fields - 1, 16, 256)] * 2 + [(fields, 4, 8, 256)] * 2 + [(fields, 16, 128)] * 2


def exchange_faces(sends):
    xlo, xhi, ylo, yhi, zlo, zhi = sends
    return both("gx", xlo, xhi) + both("gy", ylo, yhi) + both("gz", zlo, zhi)


def deep_halo(fields, m, s, xlo, xhi):
    xl, xh = both("gx", xlo, xhi)
    ylo, yhi = call(functools.partial(rows_kernel, fields), [(fields, NYT, 8, 128)] * 2, (m, s, xl, xh))
    yl, yh = both("gy", ylo, yhi)
    zlo, zhi = call(
        functools.partial(lanes_kernel, fields),
        [(fields, NZG, 8, 128)] * 2,
        (m, s, xl, xh, yl, yh),
        [(16 * NZG, 8, 128)] * 2,
    )
    zl, zh = both("gz", zlo, zhi)
    return xl, xh, yl, yh, zl, zh


def body(right_side, coefficients, first_guess):
    marks = []
    for axis in ("gx", "gy", "gz"):
        index = lax.axis_index(axis)
        marks += [index > 0, index < lax.axis_size(axis) - 1]
    m = jnp.stack(marks).astype(F32)

    sends = call(faces_kernel, face_shapes(2), (coefficients, first_guess), masked=False)
    faces = exchange_faces(sends)
    s, xlo, xhi = call(
        fields_kernel,
        [(5, NS, 8, 128)] + [(5, NXT, 8, 128)] * 2,
        (m, coefficients, first_guess, right_side) + faces,
        [(3, 512, 128)],
    )
    halo = deep_halo(5, m, s, xlo, xhi)
    weight_shapes = [(6,) + EXT[b] for b in range(3)]
    out = call(
        functools.partial(cycle_kernel, True),
        [(16, 16, 256)] + weight_shapes + face_shapes(1),
        (m, first_guess, s) + halo,
        [(16 * NZG, 8, 128), (2, 256, 128)] + [(5,) + EXT[b] for b in range(3)],
    )
    field, weights, sends = out[0], out[1:4], out[4:]
    ufaces = exchange_faces(sends)
    r, xlo, xhi = call(
        residual_kernel,
        [(1, NS, 8, 128)] + [(1, NXT, 8, 128)] * 2,
        (m, coefficients, field, right_side, s) + faces + ufaces,
        [(3, 512, 128)],
    )
    halo = deep_halo(1, m, r, xlo, xhi)
    (field,) = call(
        functools.partial(cycle_kernel, False),
        [(16, 16, 256)],
        (m, field, r) + halo + tuple(weights),
        [(16 * NZG, 8, 128), (2, 256, 128)] + [(3,) + EXT[b] for b in range(3)],
    )
    return field


def solution(mesh):
    in_specs = (P("gx", "gy", "gz"), P(None, "gx", "gy", "gz"), P("gx", "gy", "gz"))
    out_specs = P("gx", "gy", "gz")
    return jax.shard_map(body, mesh=mesh, in_specs=in_specs, out_specs=out_specs, check_vma=False)
```

```python
import functools

import jax
import jax.numpy as jnp
from jax import lax
from jax.experimental import pallas as pl
from jax.experimental.pallas import tpu as pltpu
from jax.sharding import PartitionSpec as P

CYCLES = 2
SWEEPS = 8
relaxation = 0.8
blending = 0.4

PLANES = (8, 16, 16)
HALO = (8, 7, 7)
WIDE = (24, 30, 30)
ROWT = (2, 1, 2)
LANET = (2, 2, 1)
EXT = tuple((WIDE[b], LANET[b] + 1, 8 * (ROWT[b] + 2), 128) for b in range(3))
UNROLL = 4
F32 = jnp.float32
VMEM_LIMIT = 60 * 1024 * 1024
HIGHEST = lax.Precision.HIGHEST


class Layout:
    def __init__(self, branches):
        self.branches = branches
        self.s, self.x, self.y, self.z = {}, {}, {}, {}
        ns = nx = ny = nz = 0
        for b in branches:
            self.s[b], self.x[b], self.y[b], self.z[b] = ns, nx, ny, nz
            tiles = ROWT[b] * LANET[b]
            ns += tiles * PLANES[b]
            nx += tiles * HALO[b]
            ny += LANET[b] * WIDE[b]
            nz += (ROWT[b] + 2) * WIDE[b]
        self.ns, self.nx, self.ny, self.items = ns, nx, ny, nz
        self.nz = (nz + 15) // 16


ALL = Layout((0, 1, 2))
EARLY = Layout((1, 2))
LATE = Layout((0,))


def lane_of(shape):
    return lax.broadcasted_iota(jnp.int32, shape, len(shape) - 1)


def row_of(shape):
    return lax.broadcasted_iota(jnp.int32, shape, len(shape) - 2)


def pack_rows(load):
    groups = []
    for g in range(4):
        acc = jnp.zeros((8, 256), F32)
        for j in range(4):
            value, turn = load(4 * g + j)
            turn = (turn + 2 * j) % 8
            value = pltpu.roll(value, turn, 0) if turn else value
            acc = jnp.where(row_of((8, 256)) // 2 == j, value, acc)
        groups.append(acc)
    return groups


def pack_lanes(load):
    acc = jnp.zeros((16, 128), F32)
    for j in range(16):
        value, turn = load(j)
        turn = (turn + 8 * j) % 128
        value = pltpu.roll(value, turn, 1) if turn else value
        acc = jnp.where(lane_of((16, 128)) // 8 == j, value, acc)
    return acc


def send_faces(at, row_field, lane_field, yl, yh, zl, zh):
    for g, value in enumerate(pack_rows(lambda x: (row_field(x)[0:8, :], 0))):
        yl[at, g] = value
    for g, value in enumerate(pack_rows(lambda x: (row_field(x)[8:16, :], 2))):
        yh[at, g] = value
    zl[at] = pack_lanes(lambda x: (lane_field(x)[:, 0:128], 0))
    zh[at] = pack_lanes(lambda x: (lane_field(x)[:, 128:256], 8))


def faces_kernel(k, u, xl, xh, yl, yh, zl, zh):
    xl[0:1] = u[0:1]
    xl[1:3] = k[0, 0:2]
    xh[0:1] = u[15:16]
    xh[1:3] = k[0, 14:16]
    send_faces(0, lambda x: u[x], lambda x: u[x], yl, yh, zl, zh)
    send_faces(1, lambda x: k[1, x], lambda x: k[2, x], yl, yh, zl, zh)


def halo_rows(value, at, yl, yh, m):
    high, low = [], []
    for x in range(16):
        g, j = divmod(x, 4)
        high.append(pltpu.roll(yh[at, g], (8 - 2 * j) % 8, 0) if j else yh[at, g])
        turn = (6 - 2 * j) % 8
        low.append(pltpu.roll(yl[at, g], turn, 0) if turn else yl[at, g])
    high = jnp.stack(high) * m[3]
    low = jnp.stack(low) * m[2]
    return jnp.concatenate([value, high, low], axis=1)


def halo_lanes(value, at, zl, zh, m):
    high = zh[at] * m[5]
    low = zl[at] * m[4]
    lane = lane_of((16, 128))
    tiles = []
    for x in range(16):
        a = pltpu.roll(high, (128 - 8 * x) % 128, 1) if x else high
        b = pltpu.roll(low, 120 - 8 * x, 1) if x < 15 else low
        tiles.append(jnp.where(lane < 8, a, jnp.where(lane >= 120, b, 0.0)))
    return jnp.concatenate([value, jnp.stack(tiles)], axis=2)


def up(value, axis, keep):
    return keep(pltpu.roll(value, value.shape[axis] - 1, axis))


def down(value, axis, keep):
    return keep(pltpu.roll(value, 1, axis))


def lane_means(value, lanes):
    planes, rows, width = value.shape
    source = lax.broadcasted_iota(jnp.int32, (width, lanes), 0)
    target = lax.broadcasted_iota(jnp.int32, (width, lanes), 1)
    pair = source // 2
    pair = jnp.where(source >= 320, pair + 64, pair)
    matrix = jnp.where(pair == target, jnp.float32(0.5), jnp.float32(0.0))
    out = jnp.dot(value.reshape(planes * rows, width), matrix, precision=HIGHEST, preferred_element_type=F32)
    return out.reshape(planes, rows, lanes)


def row_means(value, scratch):
    planes, rows, width = value.shape
    count = planes * rows
    parts = []
    for t in range(width // 128):
        scratch[t, 0:count] = value[:, :, 128 * t : 128 * t + 128].reshape(count, 128)
        even = scratch[t, pl.ds(0, count // 2, stride=2), :]
        odd = scratch[t, pl.ds(1, count // 2, stride=2), :]
        parts.append((0.5 * (even + odd)).reshape(planes, rows // 2, 128))
    return jnp.concatenate(parts, axis=2)


def plane_means(value):
    planes = value.shape[0]
    value = value.reshape((planes // 2, 2) + value.shape[1:])
    return 0.5 * (value[:, 0] + value[:, 1])


def residual_of(k, u, f, kfaces, ufaces, m):
    xl, xh, yl, yh, zl, zh = kfaces
    uxl, uxh, uyl, uyh, uzl, uzh = ufaces
    own, rows, lanes = (lambda v: v), (lambda v: v[:, 0:16]), (lambda v: v[:, :, 0:256])
    v = u[...]
    k0 = k[0]
    vx = jnp.concatenate([uxl[0:1] * m[0], v, uxh[0:1] * m[1]], axis=0)
    kx = jnp.concatenate([xl[2:3] * m[0], k0, xh[1:2] * m[1]], axis=0)
    total = k[3] * v
    total = total + 0.5 * (k0 + kx[2:18]) * (v - vx[2:18]) + 0.5 * (k0 + kx[0:16]) * (v - vx[0:16])
    vy = halo_rows(v, 0, uyl, uyh, m)
    k1 = k[1]
    ky = halo_rows(k1, 1, yl, yh, m)
    total = total + 0.5 * (k1 + up(ky, 1, rows)) * (v - up(vy, 1, rows))
    total = total + 0.5 * (k1 + down(ky, 1, rows)) * (v - down(vy, 1, rows))
    vz = halo_lanes(v, 0, uzl, uzh, m)
    k2 = k[2]
    kz = halo_lanes(k2, 1, zl, zh, m)
    total = total + 0.5 * (k2 + up(kz, 2, lanes)) * (v - up(vz, 2, lanes))
    total = total + 0.5 * (k2 + down(kz, 2, lanes)) * (v - down(vz, 2, lanes))
    return f[...] - total, ky, kz


def put(g, out, field, b, value):
    for yt in range(ROWT[b]):
        for lt in range(LANET[b]):
            at = g.s[b] + (yt * LANET[b] + lt) * PLANES[b]
            out[field, at : at + PLANES[b]] = value[:, 8 * yt : 8 * yt + 8, 128 * lt : 128 * lt + 128]


def put_sides(g, out, field, b, xlo, xhi):
    h, p = HALO[b], PLANES[b]
    for t in range(ROWT[b] * LANET[b]):
        to, at = g.x[b] + t * h, g.s[b] + t * p
        xlo[field, to : to + h] = out[field, at : at + h]
        xhi[field, to : to + h] = out[field, at + p - h : at + p]


def coarse_residuals(r, scratch):
    return plane_means(r), row_means(r, scratch), lane_means(r, 128)


def fields_kernel(groups, m, k, u, f, xl, xh, yl, yh, zl, zh, *outs):
    scratch = outs[-1]
    faces = (xl, xh, yl, yh, zl, zh)
    r, ky, kz = residual_of(k, u, f, faces, faces, m)
    kx = jnp.concatenate([xl[1:3] * m[0], k[0], xh[1:3] * m[1]], axis=0)
    coarse = [
        (plane_means(kx), plane_means(ky), plane_means(kz), plane_means(k[3])),
        (row_means(kx[1:19], scratch), row_means(ky, scratch), row_means(kz, scratch), row_means(k[3], scratch)),
        (lane_means(kx[1:19], 128), lane_means(ky, 128), lane_means(kz, 256), lane_means(k[3], 128)),
    ]
    residuals = coarse_residuals(r, scratch)
    for b in range(3):
        cx, cy, cz, s = coarse[b]
        p, nr, nl = PLANES[b], 8 * ROWT[b], 128 * LANET[b]
        scale = [0.5, 0.5, 0.5]
        scale[b] = 0.125
        rows, lanes = (lambda v: v[:, 0:nr]), (lambda v: v[:, :, 0:nl])
        w0l = scale[0] * (cx[1 : p + 1] + cx[0:p])
        w0h = scale[0] * (cx[1 : p + 1] + cx[2 : p + 2])
        w1l = scale[1] * (rows(cy) + down(cy, 1, rows))
        w1h = scale[1] * (rows(cy) + up(cy, 1, rows))
        w2l = scale[2] * (lanes(cz) + down(cz, 2, lanes))
        w2h = scale[2] * (lanes(cz) + up(cz, 2, lanes))
        c = relaxation / (s + w0l + w0h + w1l + w1h + w2l + w2h)
        for i, g in enumerate(groups):
            if b in g.branches:
                out, xlo, xhi = outs[3 * i : 3 * i + 3]
                for field, value in enumerate((c * residuals[b], c, w0l, w1l, w2l)):
                    put(g, out, field, b, value)
                    put_sides(g, out, field, b, xlo, xhi)


def residual_kernel(groups, m, k, u, f, *refs):
    n = len(groups)
    cs, faces, ufaces, outs, scratch = refs[:n], refs[n : n + 6], refs[n + 6 : n + 12], refs[n + 12 : -1], refs[-1]
    r, _, _ = residual_of(k, u, f, faces, ufaces, m)
    values = coarse_residuals(r, scratch)
    for i, g in enumerate(groups):
        out, xlo, xhi = outs[3 * i : 3 * i + 3]
        for b in g.branches:
            put(g, out, 0, b, values[b])
        out[0] = out[0] * cs[i][0]
        for b in g.branches:
            put_sides(g, out, 0, b, xlo, xhi)


def own_pieces(g, field, b, yt, lt, m, s, xl, xh):
    h, p = HALO[b], PLANES[b]
    t = yt * LANET[b] + lt
    at, own = g.x[b] + t * h, g.s[b] + t * p
    yield 0, h, xl[field, at : at + h] * m[0]
    yield h, p, s[field, own : own + p]
    yield h + p, h, xh[field, at : at + h] * m[1]


def pieces(g, field, b, yt, lt, m, s, xl, xh, yl, yh):
    if yt < ROWT[b]:
        yield from own_pieces(g, field, b, yt, lt, m, s, xl, xh)
        return
    at = g.y[b] + lt * WIDE[b]
    source, mask = (yh, m[3]) if yt == ROWT[b] else (yl, m[2])
    yield 0, WIDE[b], source[field, at : at + WIDE[b]] * mask


def rows_kernel(g, fields, m, s, xl, xh, *rest):
    ylo, yhi = rest[-2:]
    for field in range(fields):
        for b in g.branches:
            for lt in range(LANET[b]):
                at = g.y[b] + lt * WIDE[b]
                for x, n, value in own_pieces(g, field, b, 0, lt, m, s, xl, xh):
                    ylo[field, at + x : at + x + n] = value
                for x, n, value in own_pieces(g, field, b, ROWT[b] - 1, lt, m, s, xl, xh):
                    yhi[field, at + x : at + x + n] = value


def lanes_kernel(g, fields, m, s, xl, xh, yl, yh, *rest):
    zlo, zhi, low, high = rest[-4:]
    nz = g.nz
    lane = lane_of((nz, 8, 128))
    if g.items < 16 * nz:
        low[g.items :] = jnp.zeros((16 * nz - g.items, 8, 128), F32)
        high[g.items :] = jnp.zeros((16 * nz - g.items, 8, 128), F32)
    for field in range(fields):
        for b in g.branches:
            for yt in range(ROWT[b] + 2):
                at = g.z[b] + yt * WIDE[b]
                for x, n, value in pieces(g, field, b, yt, 0, m, s, xl, xh, yl, yh):
                    low[at + x : at + x + n] = value
                for x, n, value in pieces(g, field, b, yt, LANET[b] - 1, m, s, xl, xh, yl, yh):
                    high[at + x : at + x + n] = value
        a = jnp.zeros((nz, 8, 128), F32)
        z = jnp.zeros((nz, 8, 128), F32)
        for j in range(16):
            v = low[nz * j : nz * j + nz]
            a = jnp.where(lane // 8 == j, pltpu.roll(v, 8 * j, 2) if j else v, a)
            v = high[nz * j : nz * j + nz]
            z = jnp.where(lane // 8 == j, pltpu.roll(v, 8 * j + 8, 2) if j < 15 else v, z)
        zlo[field] = a
        zhi[field] = z


def assemble(g, field, m, s, xl, xh, yl, yh, zl, zh, halo, ext):
    nz = g.nz
    lane = lane_of((nz, 8, 128))
    high = zh[field] * m[5]
    low = zl[field] * m[4]
    for j in range(16):
        a = pltpu.roll(high, 128 - 8 * j, 2) if j else high
        b = pltpu.roll(low, 120 - 8 * j, 2) if j < 15 else low
        halo[nz * j : nz * j + nz] = jnp.where(lane < 8, a, jnp.where(lane >= 120, b, 0.0))
    for b in g.branches:
        out = ext[b][field]
        for yt in range(ROWT[b] + 2):
            for lt in range(LANET[b]):
                for x, n, value in pieces(g, field, b, yt, lt, m, s, xl, xh, yl, yh):
                    out[x : x + n, lt, 8 * yt : 8 * yt + 8, :] = value
            at = g.z[b] + yt * WIDE[b]
            out[:, LANET[b], 8 * yt : 8 * yt + 8, :] = halo[at : at + WIDE[b]]


def lane_shifted(tiles, lane):
    n = len(tiles)
    below = [pltpu.roll(v, 1, 1) for v in tiles]
    above = [pltpu.roll(v, 127, 1) for v in tiles]
    below = [jnp.where(lane == 0, below[t - 1], below[t]) for t in range(n)]
    above = [jnp.where(lane == 127, above[(t + 1) % n], above[t]) for t in range(n)]
    return below, above


def scaled_weights(b, ext, weights):
    wide, lanes, rows, _ = EXT[b]
    lane = lane_of((rows, 128))
    _, c_ref, w0_ref, w1_ref, w2_ref = ext

    def plane(x, carry):
        _, above = lane_shifted([w2_ref[x, t] for t in range(lanes)], lane)
        for t in range(lanes):
            c, w1 = c_ref[x, t], w1_ref[x, t]
            weights[0, x, t] = c * w0_ref[x, t]
            weights[1, x, t] = c * w0_ref[x + 1, t]
            weights[2, x, t] = c * w1
            weights[3, x, t] = c * pltpu.roll(w1, rows - 1, 0)
            weights[4, x, t] = c * w2_ref[x, t]
            weights[5, x, t] = c * above[t]
        return carry

    lax.fori_loop(1, wide - 1, plane, 0)
    for x in (0, wide - 1):
        weights[:, x] = jnp.zeros((6, lanes, rows, 128), F32)


def sweeps(b, bias, slots, weights):
    wide, lanes, rows, _ = EXT[b]
    lane = lane_of((rows, 128))

    def plane(x, source):
        tiles = [source[x, t] for t in range(lanes)]
        below, above = lane_shifted(tiles, lane)
        outs = []
        for t, e in enumerate(tiles):
            total = bias[x, t] + (1.0 - relaxation) * e
            total = total + (weights[0, x, t] * source[x - 1, t] + weights[1, x, t] * source[x + 1, t])
            total = total + (weights[2, x, t] * pltpu.roll(e, 1, 0) + weights[3, x, t] * pltpu.roll(e, rows - 1, 0))
            total = total + (weights[4, x, t] * below[t] + weights[5, x, t] * above[t])
            outs.append(total)
        return outs

    source = bias
    for sweep in range(1, SWEEPS):
        target = slots[0] if source is not slots[0] else slots[1]

        def planes(start, count, source=source, target=target):
            outs = [plane(start + i, source) for i in range(count)]
            for i, tiles in enumerate(outs):
                for t, total in enumerate(tiles):
                    target[start + i, t] = total

        def step(i, carry, sweep=sweep, planes=planes):
            planes(sweep + i * UNROLL, UNROLL)
            return carry

        count = wide - 2 * sweep
        lax.fori_loop(0, count // UNROLL, step, 0)
        if count % UNROLL:
            planes(sweep + count - count % UNROLL, count % UNROLL)
        source = target
    return source


def correction_rows(e, joined):
    for x in range(16):
        for t in range(2):
            v = e[7 + x, t]
            even = 0.75 * v + 0.25 * pltpu.roll(v, 1, 0)
            odd = 0.75 * v + 0.25 * pltpu.roll(v, 23, 0)
            joined[t, pl.ds(16 * x, 8, stride=2), :] = even[0:8]
            joined[t, pl.ds(16 * x + 1, 8, stride=2), :] = odd[0:8]
    return jnp.concatenate([joined[0], joined[1]], axis=1).reshape(16, 16, 256)


def correction_lanes(e):
    source = lax.broadcasted_iota(jnp.int32, (256, 256), 0)
    target = lax.broadcasted_iota(jnp.int32, (256, 256), 1)
    near = target // 2
    far = (near + 2 * (target % 2) - 1 + 256) % 256
    matrix = jnp.where(source == near, 0.75, jnp.where(source == far, 0.25, 0.0)).astype(F32)
    values = jnp.concatenate([e[7:23, 0, 0:16, :], e[7:23, 1, 0:16, :]], axis=2).reshape(256, 256)
    out = jnp.dot(values, matrix, precision=HIGHEST, preferred_element_type=F32)
    return out.reshape(16, 16, 256)


def correction_planes(e):
    parts = []
    for t in range(2):
        middle, low, high = (e[i : i + 8, t, 0:16, :] for i in (8, 7, 9))
        even = 0.75 * middle + 0.25 * low
        odd = 0.75 * middle + 0.25 * high
        parts.append(jnp.stack([even, odd], axis=1).reshape(16, 16, 128))
    return jnp.concatenate(parts, axis=2)


def cycle_kernel(g, first, final, sends, *refs):
    refs = list(refs)

    def take(n):
        head = refs[:n]
        del refs[:n]
        return head

    n = len(g.branches)
    m, s, xl, xh, yl, yh, zl, zh = take(8)
    u = take(1)[0] if final else None
    other = take(1)[0] if final and n < 3 else None
    stored = take(n) if not first else None
    (out,) = take(1)
    if first:
        stored = take(n)
    face_outs = take(6) if sends else None
    halo, joined, sem = take(3)
    weights = dict(zip(g.branches, take(n)))
    ext = {b: take(5 if first else 3) for b in g.branches}

    def copy(i, b):
        ends = (weights[b], stored[i]) if first else (stored[i], weights[b])
        return pltpu.make_async_copy(*ends, sem.at[i])

    if not first:
        for i, b in enumerate(g.branches):
            copy(i, b).start()
    for field in range(5 if first else 1):
        assemble(g, field, m, s, xl, xh, yl, yh, zl, zh, halo, ext)
    last = {}
    for i, b in enumerate(g.branches):
        if first:
            scaled_weights(b, ext[b], weights[b])
            copy(i, b).start()
        else:
            copy(i, b).wait()
        last[b] = sweeps(b, ext[b][0], ext[b][1:3], weights[b])
    total = other[...] if other is not None else None
    for b in g.branches:
        part = (correction_planes, lambda e: correction_rows(e, joined), correction_lanes)[b](last[b])
        total = part if total is None else total + part
    out[...] = u[...] + blending * total if final else total
    if sends:
        uxlo, uxhi, uylo, uyhi, uzlo, uzhi = face_outs
        uxlo[0:1] = out[0:1]
        uxhi[0:1] = out[15:16]
        send_faces(0, lambda x: out[x], lambda x: out[x], uylo, uyhi, uzlo, uzhi)
    if first:
        for i, b in enumerate(g.branches):
            copy(i, b).wait()


def ring(value, axis, step):
    n = lax.axis_size(axis)
    return lax.ppermute(value, axis, [(i, (i + step) % n) for i in range(n)])


def both(axis, to_low, to_high):
    return ring(to_high, axis, 1), ring(to_low, axis, -1)


def call(kernel, outs, args, scratch=(), masked=True, away=0, away_outs=()):
    vmem, anywhere = pl.BlockSpec(memory_space=pltpu.VMEM), pl.BlockSpec(memory_space=pl.ANY)
    specs = [vmem] * (len(args) - away) + [anywhere] * away
    if masked:
        specs[0] = pl.BlockSpec(memory_space=pltpu.SMEM)
    return pl.pallas_call(
        kernel,
        out_shape=[jax.ShapeDtypeStruct(shape, F32) for shape in outs],
        in_specs=specs,
        out_specs=[anywhere if i in away_outs else vmem for i in range(len(outs))],
        scratch_shapes=[pltpu.VMEM(shape, F32) if isinstance(shape, tuple) else shape for shape in scratch],
        compiler_params=pltpu.CompilerParams(vmem_limit_bytes=VMEM_LIMIT),
    )(*args)


def face_shapes(fields):
    return [(2 * fields - 1, 16, 256)] * 2 + [(fields, 4, 8, 256)] * 2 + [(fields, 16, 128)] * 2


def exchange_faces(sends):
    xlo, xhi, ylo, yhi, zlo, zhi = sends
    return both("gx", xlo, xhi) + both("gy", ylo, yhi) + both("gz", zlo, zhi)


def rows_exchange(g, fields, m, s, xl, xh, after=()):
    ylo, yhi = call(
        functools.partial(rows_kernel, g, fields),
        [(fields, g.ny, 8, 128)] * 2,
        (m, s, xl, xh) + tuple(after),
        away=len(after),
    )
    return both("gy", ylo, yhi), ylo


def lanes_exchange(g, fields, m, s, xl, xh, yl, yh, after=()):
    zlo, zhi = call(
        functools.partial(lanes_kernel, g, fields),
        [(fields, g.nz, 8, 128)] * 2,
        (m, s, xl, xh, yl, yh) + tuple(after),
        [(16 * g.nz, 8, 128)] * 2,
        away=len(after),
    )
    return both("gz", zlo, zhi)


def weight_shape(b):
    return (6,) + EXT[b]


def cycle(g, first, final, sends, args, weights=()):
    outs = [(16, 16, 256)]
    if first:
        outs += [weight_shape(b) for b in g.branches]
    away_outs = range(1, len(outs))
    if sends:
        outs += face_shapes(1)
    scratch = [(16 * g.nz, 8, 128), (2, 256, 128), pltpu.SemaphoreType.DMA((len(g.branches),))]
    scratch += [weight_shape(b) for b in g.branches]
    for b in g.branches:
        scratch += [EXT[b]] * (5 if first else 3)
    kernel = functools.partial(cycle_kernel, g, first, final, sends)
    return call(kernel, outs, args + tuple(weights), scratch, away=len(weights), away_outs=away_outs)


def group_shapes(groups, fields):
    shapes = []
    for g in groups:
        shapes += [(fields, g.ns, 8, 128)] + [(fields, g.nx, 8, 128)] * 2
    return shapes


def body(right_side, coefficients, first_guess):
    marks = []
    for axis in ("gx", "gy", "gz"):
        index = lax.axis_index(axis)
        marks += [index > 0, index < lax.axis_size(axis) - 1]
    m = jnp.stack(marks).astype(F32)

    sends = call(faces_kernel, face_shapes(2), (coefficients, first_guess), masked=False)
    faces = exchange_faces(sends)
    groups = (EARLY, LATE)
    s1, xlo1, xhi1, s0, xlo0, xhi0 = call(
        functools.partial(fields_kernel, groups),
        group_shapes(groups, 5),
        (m, coefficients, first_guess, right_side) + faces,
        [(3, 512, 128)],
    )
    x1 = both("gx", xlo1, xhi1)
    x0 = both("gx", xlo0, xhi0)
    y1, mark = rows_exchange(EARLY, 5, m, s1, *x1)
    y0, mark = rows_exchange(LATE, 5, m, s0, *x0, after=(mark,))
    z1 = lanes_exchange(EARLY, 5, m, s1, *x1, *y1, after=(mark,))
    partial, weights1, weights2 = cycle(EARLY, True, False, False, (m, s1) + x1 + y1 + z1)
    z0 = lanes_exchange(LATE, 5, m, s0, *x0, *y0)
    out = cycle(LATE, True, True, True, (m, s0) + x0 + y0 + z0 + (first_guess, partial))
    field, weights0, sends = out[0], out[1], out[2:]

    ufaces = exchange_faces(sends)
    c = jnp.concatenate([s0[1:2], s1[1:2]], axis=1)
    r, xlo, xhi = call(
        functools.partial(residual_kernel, (ALL,)),
        group_shapes((ALL,), 1),
        (m, coefficients, field, right_side, c) + faces + ufaces,
        [(3, 512, 128)],
    )
    x = both("gx", xlo, xhi)
    y, _ = rows_exchange(ALL, 1, m, r, *x)
    z = lanes_exchange(ALL, 1, m, r, *x, *y)
    (field,) = cycle(ALL, False, True, False, (m, r) + x + y + z + (field,), (weights0, weights1, weights2))
    return field


def solution(mesh):
    in_specs = (P("gx", "gy", "gz"), P(None, "gx", "gy", "gz"), P("gx", "gy", "gz"))
    out_specs = P("gx", "gy", "gz")
    return jax.shard_map(body, mesh=mesh, in_specs=in_specs, out_specs=out_specs, check_vma=False)
```

```python
import functools

import jax
import jax.numpy as jnp
from jax import lax
from jax.experimental import pallas as pl
from jax.experimental.pallas import tpu as pltpu
from jax.sharding import PartitionSpec as P

CYCLES = 2
SWEEPS = 8
relaxation = 0.8
blending = 0.4

PLANES = (8, 16, 16)
HALO = (8, 7, 7)
WIDE = (24, 30, 30)
ROWT = (2, 1, 2)
LANET = (2, 2, 1)
EXT = tuple((WIDE[b], LANET[b] + 1, 8 * (ROWT[b] + 2), 128) for b in range(3))
UNROLL = 4
F32 = jnp.float32
VMEM_LIMIT = 60 * 1024 * 1024
HIGHEST = lax.Precision.HIGHEST


class Layout:
    def __init__(self, branches, fields):
        self.branches, self.fields = branches, fields
        self.s, self.z, self.x, self.own, self.corner = {}, {}, {}, {}, {}
        ns = nz = nx = no = nc = 0
        for b in branches:
            self.s[b], self.z[b] = ns, nz
            ns += ROWT[b] * LANET[b] * PLANES[b]
            nz += (ROWT[b] + 2) * WIDE[b]
        for f in range(fields):
            for b in branches:
                self.x[f, b], self.own[f, b], self.corner[f, b] = nx, no, nc
                nx += ROWT[b] * LANET[b] * depth(f, b)
                no += LANET[b] * PLANES[b]
                nc += LANET[b] * 2 * depth(f, b)
        self.ns, self.nx, self.no, self.nc, self.items = ns, nx, no, nc, nz
        self.nz = (nz + 15) // 16


def depth(field, b):
    return HALO[b] - (field in (1, 3, 4))


ALL = Layout((0, 1, 2), 1)
OWN = Layout((0, 1, 2), 5)
EARLY = Layout((1, 2), 5)
LATE = Layout((0,), 5)


def lane_of(shape):
    return lax.broadcasted_iota(jnp.int32, shape, len(shape) - 1)


def row_of(shape):
    return lax.broadcasted_iota(jnp.int32, shape, len(shape) - 2)


def pack_rows(load):
    groups = []
    for g in range(4):
        acc = jnp.zeros((8, 256), F32)
        for j in range(4):
            value, turn = load(4 * g + j)
            turn = (turn + 2 * j) % 8
            value = pltpu.roll(value, turn, 0) if turn else value
            acc = jnp.where(row_of((8, 256)) // 2 == j, value, acc)
        groups.append(acc)
    return groups


def pack_lanes(load):
    acc = jnp.zeros((16, 128), F32)
    for j in range(16):
        value, turn = load(j)
        turn = (turn + 8 * j) % 128
        value = pltpu.roll(value, turn, 1) if turn else value
        acc = jnp.where(lane_of((16, 128)) // 8 == j, value, acc)
    return acc


def send_faces(at, row_field, lane_field, yl, yh, zl, zh):
    for g, value in enumerate(pack_rows(lambda x: (row_field(x)[0:8, :], 0))):
        yl[at, g] = value
    for g, value in enumerate(pack_rows(lambda x: (row_field(x)[8:16, :], 2))):
        yh[at, g] = value
    zl[at] = pack_lanes(lambda x: (lane_field(x)[:, 0:128], 0))
    zh[at] = pack_lanes(lambda x: (lane_field(x)[:, 128:256], 8))


def faces_kernel(k, u, xl, xh, yl, yh, zl, zh):
    xl[0:1] = u[0:1]
    xl[1:3] = k[0, 0:2]
    xh[0:1] = u[15:16]
    xh[1:3] = k[0, 14:16]
    send_faces(0, lambda x: u[x], lambda x: u[x], yl, yh, zl, zh)
    send_faces(1, lambda x: k[1, x], lambda x: k[2, x], yl, yh, zl, zh)


def halo_rows(value, at, yl, yh, m):
    high, low = [], []
    for x in range(16):
        g, j = divmod(x, 4)
        high.append(pltpu.roll(yh[at, g], (8 - 2 * j) % 8, 0) if j else yh[at, g])
        turn = (6 - 2 * j) % 8
        low.append(pltpu.roll(yl[at, g], turn, 0) if turn else yl[at, g])
    high = jnp.stack(high) * m[3]
    low = jnp.stack(low) * m[2]
    return jnp.concatenate([value, high, low], axis=1)


def halo_lanes(value, at, zl, zh, m):
    high = zh[at] * m[5]
    low = zl[at] * m[4]
    lane = lane_of((16, 128))
    tiles = []
    for x in range(16):
        a = pltpu.roll(high, (128 - 8 * x) % 128, 1) if x else high
        b = pltpu.roll(low, 120 - 8 * x, 1) if x < 15 else low
        tiles.append(jnp.where(lane < 8, a, jnp.where(lane >= 120, b, 0.0)))
    return jnp.concatenate([value, jnp.stack(tiles)], axis=2)


def up(value, axis, keep):
    return keep(pltpu.roll(value, value.shape[axis] - 1, axis))


def down(value, axis, keep):
    return keep(pltpu.roll(value, 1, axis))


def lane_means(value, lanes):
    planes, rows, width = value.shape
    source = lax.broadcasted_iota(jnp.int32, (width, lanes), 0)
    target = lax.broadcasted_iota(jnp.int32, (width, lanes), 1)
    pair = source // 2
    pair = jnp.where(source >= 320, pair + 64, pair)
    matrix = jnp.where(pair == target, jnp.float32(0.5), jnp.float32(0.0))
    out = jnp.dot(value.reshape(planes * rows, width), matrix, precision=HIGHEST, preferred_element_type=F32)
    return out.reshape(planes, rows, lanes)


def row_means(value, scratch):
    planes, rows, width = value.shape
    count = planes * rows
    parts = []
    for t in range(width // 128):
        scratch[t, 0:count] = value[:, :, 128 * t : 128 * t + 128].reshape(count, 128)
        even = scratch[t, pl.ds(0, count // 2, stride=2), :]
        odd = scratch[t, pl.ds(1, count // 2, stride=2), :]
        parts.append((0.5 * (even + odd)).reshape(planes, rows // 2, 128))
    return jnp.concatenate(parts, axis=2)


def plane_means(value):
    planes = value.shape[0]
    value = value.reshape((planes // 2, 2) + value.shape[1:])
    return 0.5 * (value[:, 0] + value[:, 1])


def residual_of(k, u, f, kfaces, ufaces, m):
    xl, xh, yl, yh, zl, zh = kfaces
    uxl, uxh, uyl, uyh, uzl, uzh = ufaces
    own, rows, lanes = (lambda v: v), (lambda v: v[:, 0:16]), (lambda v: v[:, :, 0:256])
    v = u[...]
    k0 = k[0]
    vx = jnp.concatenate([uxl[0:1] * m[0], v, uxh[0:1] * m[1]], axis=0)
    kx = jnp.concatenate([xl[2:3] * m[0], k0, xh[1:2] * m[1]], axis=0)
    total = k[3] * v
    total = total + 0.5 * (k0 + kx[2:18]) * (v - vx[2:18]) + 0.5 * (k0 + kx[0:16]) * (v - vx[0:16])
    vy = halo_rows(v, 0, uyl, uyh, m)
    k1 = k[1]
    ky = halo_rows(k1, 1, yl, yh, m)
    total = total + 0.5 * (k1 + up(ky, 1, rows)) * (v - up(vy, 1, rows))
    total = total + 0.5 * (k1 + down(ky, 1, rows)) * (v - down(vy, 1, rows))
    vz = halo_lanes(v, 0, uzl, uzh, m)
    k2 = k[2]
    kz = halo_lanes(k2, 1, zl, zh, m)
    total = total + 0.5 * (k2 + up(kz, 2, lanes)) * (v - up(vz, 2, lanes))
    total = total + 0.5 * (k2 + down(kz, 2, lanes)) * (v - down(vz, 2, lanes))
    return f[...] - total, ky, kz


def put(g, out, field, b, value):
    for yt in range(ROWT[b]):
        for lt in range(LANET[b]):
            at = g.s[b] + (yt * LANET[b] + lt) * PLANES[b]
            out[field, at : at + PLANES[b]] = value[:, 8 * yt : 8 * yt + 8, 128 * lt : 128 * lt + 128]


def put_sides(g, out, field, b, xlo, xhi):
    h, p = depth(field, b), PLANES[b]
    for t in range(ROWT[b] * LANET[b]):
        to, at = g.x[field, b] + t * h, g.s[b] + t * p
        xlo[to : to + h] = out[field, at : at + h]
        xhi[to : to + h] = out[field, at + p - h : at + p]


def put_own_rows(g, to, out, field, b, ylo, yhi):
    p = PLANES[b]
    for lt in range(LANET[b]):
        at, first = to.own[field, b] + lt * p, g.s[b] + lt * p
        last = first + (ROWT[b] - 1) * LANET[b] * p
        ylo[at : at + p] = out[field, first : first + p]
        yhi[at : at + p] = out[field, last : last + p]


def coarse_residuals(r, scratch):
    return plane_means(r), row_means(r, scratch), lane_means(r, 128)


def fields_kernel(groups, m, k, u, f, xl, xh, yl, yh, zl, zh, *outs):
    scratch = outs[-1]
    faces = (xl, xh, yl, yh, zl, zh)
    r, ky, kz = residual_of(k, u, f, faces, faces, m)
    kx = jnp.concatenate([xl[1:3] * m[0], k[0], xh[1:3] * m[1]], axis=0)
    coarse = [
        (plane_means(kx), plane_means(ky), plane_means(kz), plane_means(k[3])),
        (row_means(kx[1:19], scratch), row_means(ky, scratch), row_means(kz, scratch), row_means(k[3], scratch)),
        (lane_means(kx[1:19], 128), lane_means(ky, 128), lane_means(kz, 256), lane_means(k[3], 128)),
    ]
    residuals = coarse_residuals(r, scratch)
    ylo, yhi, kept = outs[3 * len(groups) : 3 * len(groups) + 3]
    for b in range(3):
        cx, cy, cz, s = coarse[b]
        p, nr, nl = PLANES[b], 8 * ROWT[b], 128 * LANET[b]
        scale = [0.5, 0.5, 0.5]
        scale[b] = 0.125
        rows, lanes = (lambda v: v[:, 0:nr]), (lambda v: v[:, :, 0:nl])
        w0l = scale[0] * (cx[1 : p + 1] + cx[0:p])
        w0h = scale[0] * (cx[1 : p + 1] + cx[2 : p + 2])
        w1l = scale[1] * (rows(cy) + down(cy, 1, rows))
        w1h = scale[1] * (rows(cy) + up(cy, 1, rows))
        w2l = scale[2] * (lanes(cz) + down(cz, 2, lanes))
        w2h = scale[2] * (lanes(cz) + up(cz, 2, lanes))
        c = relaxation / (s + w0l + w0h + w1l + w1h + w2l + w2h)
        for i, g in enumerate(groups):
            if b in g.branches:
                out, xlo, xhi = outs[3 * i : 3 * i + 3]
                for field, value in enumerate((c * residuals[b], c, w0l, w1l, w2l)):
                    put(g, out, field, b, value)
                    put_sides(g, out, field, b, xlo, xhi)
                    put_own_rows(g, OWN, out, field, b, ylo, yhi)
        put(ALL, kept, 0, b, c)


def residual_kernel(g, m, k, u, f, c, *refs):
    faces, ufaces, (out, xlo, xhi, ylo, yhi, scratch) = refs[:6], refs[6:12], refs[12:]
    r, _, _ = residual_of(k, u, f, faces, ufaces, m)
    values = coarse_residuals(r, scratch)
    for b in g.branches:
        put(g, out, 0, b, values[b])
    out[...] = out[...] * c[...]
    for b in g.branches:
        put_sides(g, out, 0, b, xlo, xhi)
        put_own_rows(g, g, out, 0, b, ylo, yhi)


def pieces(g, own, field, b, yt, lt, m, s, xl, xh, yol, yoh, ycl, ych):
    h, p, hf = HALO[b], PLANES[b], depth(field, b)
    if yt < ROWT[b]:
        t = yt * LANET[b] + lt
        at, first = g.x[field, b] + t * hf, g.s[b] + t * p
        yield h - hf, hf, xl[at : at + hf] * m[0]
        yield h, p, s[field, first : first + p]
        yield h + p, hf, xh[at : at + hf] * m[1]
        return
    inner, outer, mask = (yoh, ych, m[3]) if yt == ROWT[b] else (yol, ycl, m[2])
    at, first = g.corner[field, b] + lt * 2 * hf, own.own[field, b] + lt * p
    yield h - hf, hf, outer[at : at + hf] * mask
    yield h, p, inner[first : first + p] * mask
    yield h + p, hf, outer[at + hf : at + 2 * hf] * mask


def corners_kernel(g, m, xl, xh, *rest):
    ylo, yhi = rest[-2:]
    for field in range(g.fields):
        for b in g.branches:
            h = depth(field, b)
            for lt in range(LANET[b]):
                to = g.corner[field, b] + lt * 2 * h
                at = g.x[field, b] + lt * h
                last = at + (ROWT[b] - 1) * LANET[b] * h
                ylo[to : to + h] = xl[at : at + h] * m[0]
                ylo[to + h : to + 2 * h] = xh[at : at + h] * m[1]
                yhi[to : to + h] = xl[last : last + h] * m[0]
                yhi[to + h : to + 2 * h] = xh[last : last + h] * m[1]


def lanes_kernel(g, own, m, *rest):
    arrays = rest[:7]
    zlo, zhi, low, high = rest[-4:]
    nz = g.nz
    lane = lane_of((nz, 8, 128))
    if g.items < 16 * nz:
        low[g.items :] = jnp.zeros((16 * nz - g.items, 8, 128), F32)
        high[g.items :] = jnp.zeros((16 * nz - g.items, 8, 128), F32)
    for field in range(g.fields):
        for b in g.branches:
            for yt in range(ROWT[b] + 2):
                at = g.z[b] + yt * WIDE[b]
                for x, n, value in pieces(g, own, field, b, yt, 0, m, *arrays):
                    low[at + x : at + x + n] = value
                for x, n, value in pieces(g, own, field, b, yt, LANET[b] - 1, m, *arrays):
                    high[at + x : at + x + n] = value
        a = jnp.zeros((nz, 8, 128), F32)
        z = jnp.zeros((nz, 8, 128), F32)
        for j in range(16):
            v = low[nz * j : nz * j + nz]
            a = jnp.where(lane // 8 == j, pltpu.roll(v, 8 * j, 2) if j else v, a)
            v = high[nz * j : nz * j + nz]
            z = jnp.where(lane // 8 == j, pltpu.roll(v, 8 * j + 8, 2) if j < 15 else v, z)
        zlo[field] = a
        zhi[field] = z


def assemble(g, own, field, m, arrays, zl, zh, halo, ext):
    nz = g.nz
    lane = lane_of((nz, 8, 128))
    high = zh[field] * m[5]
    low = zl[field] * m[4]
    for j in range(16):
        a = pltpu.roll(high, 128 - 8 * j, 2) if j else high
        b = pltpu.roll(low, 120 - 8 * j, 2) if j < 15 else low
        halo[nz * j : nz * j + nz] = jnp.where(lane < 8, a, jnp.where(lane >= 120, b, 0.0))
    for b in g.branches:
        out = ext[b][field]
        for yt in range(ROWT[b] + 2):
            for lt in range(LANET[b]):
                for x, n, value in pieces(g, own, field, b, yt, lt, m, *arrays):
                    out[x : x + n, lt, 8 * yt : 8 * yt + 8, :] = value
            at = g.z[b] + yt * WIDE[b]
            out[:, LANET[b], 8 * yt : 8 * yt + 8, :] = halo[at : at + WIDE[b]]


def lane_shifted(tiles, lane):
    n = len(tiles)
    below = [pltpu.roll(v, 1, 1) for v in tiles]
    above = [pltpu.roll(v, 127, 1) for v in tiles]
    below = [jnp.where(lane == 0, below[t - 1], below[t]) for t in range(n)]
    above = [jnp.where(lane == 127, above[(t + 1) % n], above[t]) for t in range(n)]
    return below, above


def scaled_weights(b, ext, weights):
    wide, lanes, rows, _ = EXT[b]
    lane = lane_of((rows, 128))
    _, c_ref, w0_ref, w1_ref, w2_ref = ext

    def plane(x):
        w2 = [w2_ref[x, t] for t in range(lanes)]
        _, above = lane_shifted(w2, lane)
        outs = []
        for t in range(lanes):
            c, w1 = c_ref[x, t], w1_ref[x, t]
            sides = (w0_ref[x, t], w0_ref[x + 1, t], w1, pltpu.roll(w1, rows - 1, 0), w2[t], above[t])
            outs.append([c * v for v in sides])
        return outs

    def step(i, carry):
        outs = [plane(1 + 2 * i + j) for j in range(2)]
        for j, tiles in enumerate(outs):
            for t, values in enumerate(tiles):
                for side, value in enumerate(values):
                    weights[side, 1 + 2 * i + j, t] = value
        return carry

    lax.fori_loop(0, (wide - 2) // 2, step, 0)
    for x in (0, wide - 1):
        weights[:, x] = jnp.zeros((6, lanes, rows, 128), F32)


def sweeps(b, bias, slots, weights):
    wide, lanes, rows, _ = EXT[b]
    lane = lane_of((rows, 128))

    def plane(x, source):
        tiles = [source[x, t] for t in range(lanes)]
        below, above = lane_shifted(tiles, lane)
        outs = []
        for t, e in enumerate(tiles):
            total = bias[x, t] + (1.0 - relaxation) * e
            total = total + (weights[0, x, t] * source[x - 1, t] + weights[1, x, t] * source[x + 1, t])
            total = total + (weights[2, x, t] * pltpu.roll(e, 1, 0) + weights[3, x, t] * pltpu.roll(e, rows - 1, 0))
            total = total + (weights[4, x, t] * below[t] + weights[5, x, t] * above[t])
            outs.append(total)
        return outs

    source = bias
    for sweep in range(1, SWEEPS):
        target = slots[0] if source is not slots[0] else slots[1]

        def planes(start, count, source=source, target=target):
            outs = [plane(start + i, source) for i in range(count)]
            for i, tiles in enumerate(outs):
                for t, total in enumerate(tiles):
                    target[start + i, t] = total

        def step(i, carry, sweep=sweep, planes=planes):
            planes(sweep + i * UNROLL, UNROLL)
            return carry

        count = wide - 2 * sweep
        lax.fori_loop(0, count // UNROLL, step, 0)
        if count % UNROLL:
            planes(sweep + count - count % UNROLL, count % UNROLL)
        source = target
    return source


def correction_rows(e, joined):
    for x in range(16):
        for t in range(2):
            v = e[7 + x, t]
            even = 0.75 * v + 0.25 * pltpu.roll(v, 1, 0)
            odd = 0.75 * v + 0.25 * pltpu.roll(v, 23, 0)
            joined[t, pl.ds(16 * x, 8, stride=2), :] = even[0:8]
            joined[t, pl.ds(16 * x + 1, 8, stride=2), :] = odd[0:8]
    return jnp.concatenate([joined[0], joined[1]], axis=1).reshape(16, 16, 256)


def correction_lanes(e):
    source = lax.broadcasted_iota(jnp.int32, (256, 256), 0)
    target = lax.broadcasted_iota(jnp.int32, (256, 256), 1)
    near = target // 2
    far = (near + 2 * (target % 2) - 1 + 256) % 256
    matrix = jnp.where(source == near, 0.75, jnp.where(source == far, 0.25, 0.0)).astype(F32)
    values = jnp.concatenate([e[7:23, 0, 0:16, :], e[7:23, 1, 0:16, :]], axis=2).reshape(256, 256)
    out = jnp.dot(values, matrix, precision=HIGHEST, preferred_element_type=F32)
    return out.reshape(16, 16, 256)


def correction_planes(e):
    parts = []
    for t in range(2):
        middle, low, high = (e[i : i + 8, t, 0:16, :] for i in (8, 7, 9))
        even = 0.75 * middle + 0.25 * low
        odd = 0.75 * middle + 0.25 * high
        parts.append(jnp.stack([even, odd], axis=1).reshape(16, 16, 128))
    return jnp.concatenate(parts, axis=2)


def cycle_kernel(g, own, first, final, sends, *refs):
    refs = list(refs)

    def take(n):
        head = refs[:n]
        del refs[:n]
        return head

    n = len(g.branches)
    (m,) = take(1)
    arrays = take(7)
    zl, zh = take(2)
    u = take(1)[0] if final else None
    other = take(1)[0] if final and n < 3 else None
    stored = take(n) if not first else None
    (out,) = take(1)
    if first:
        stored = take(n)
    face_outs = take(6) if sends else None
    halo, joined, sem = take(3)
    weights = dict(zip(g.branches, take(n)))
    ext = {b: take(5 if first else 3) for b in g.branches}

    def copy(i, b):
        ends = (weights[b], stored[i]) if first else (stored[i], weights[b])
        return pltpu.make_async_copy(*ends, sem.at[i])

    if not first:
        for i, b in enumerate(g.branches):
            copy(i, b).start()
    for field in range(5 if first else 1):
        assemble(g, own, field, m, arrays, zl, zh, halo, ext)
    last = {}
    for i, b in enumerate(g.branches):
        if first:
            scaled_weights(b, ext[b], weights[b])
            copy(i, b).start()
        else:
            copy(i, b).wait()
        last[b] = sweeps(b, ext[b][0], ext[b][1:3], weights[b])
    total = other[...] if other is not None else None
    for b in g.branches:
        part = (correction_planes, lambda e: correction_rows(e, joined), correction_lanes)[b](last[b])
        total = part if total is None else total + part
    out[...] = u[...] + blending * total if final else total
    if sends:
        uxlo, uxhi, uylo, uyhi, uzlo, uzhi = face_outs
        uxlo[0:1] = out[0:1]
        uxhi[0:1] = out[15:16]
        send_faces(0, lambda x: out[x], lambda x: out[x], uylo, uyhi, uzlo, uzhi)
    if first:
        for i, b in enumerate(g.branches):
            copy(i, b).wait()


def ring(value, axis, step):
    n = lax.axis_size(axis)
    return lax.ppermute(value, axis, [(i, (i + step) % n) for i in range(n)])


def both(axis, to_low, to_high):
    return ring(to_high, axis, 1), ring(to_low, axis, -1)


def call(kernel, outs, args, scratch=(), masked=True, away=0, away_outs=()):
    vmem, anywhere = pl.BlockSpec(memory_space=pltpu.VMEM), pl.BlockSpec(memory_space=pl.ANY)
    specs = [vmem] * (len(args) - away) + [anywhere] * away
    if masked:
        specs[0] = pl.BlockSpec(memory_space=pltpu.SMEM)
    return pl.pallas_call(
        kernel,
        out_shape=[jax.ShapeDtypeStruct(shape, F32) for shape in outs],
        in_specs=specs,
        out_specs=[anywhere if i in away_outs else vmem for i in range(len(outs))],
        scratch_shapes=[pltpu.VMEM(shape, F32) if isinstance(shape, tuple) else shape for shape in scratch],
        compiler_params=pltpu.CompilerParams(vmem_limit_bytes=VMEM_LIMIT),
    )(*args)


def face_shapes(fields):
    return [(2 * fields - 1, 16, 256)] * 2 + [(fields, 4, 8, 256)] * 2 + [(fields, 16, 128)] * 2


def exchange_faces(sends):
    xlo, xhi, ylo, yhi, zlo, zhi = sends
    return both("gx", xlo, xhi) + both("gy", ylo, yhi) + both("gz", zlo, zhi)


def corners_exchange(g, m, xl, xh, after=()):
    ylo, yhi = call(
        functools.partial(corners_kernel, g),
        [(g.nc, 8, 128)] * 2,
        (m, xl, xh) + tuple(after),
        away=len(after),
    )
    return both("gy", ylo, yhi), ylo


def lanes_exchange(g, own, m, arrays, after=()):
    zlo, zhi = call(
        functools.partial(lanes_kernel, g, own),
        [(g.fields, g.nz, 8, 128)] * 2,
        (m,) + arrays + tuple(after),
        [(16 * g.nz, 8, 128)] * 2,
        away=len(after),
    )
    return both("gz", zlo, zhi), zlo


def weight_shape(b):
    return (6,) + EXT[b]


def cycle(g, own, first, final, sends, args, weights=()):
    outs = [(16, 16, 256)]
    if first:
        outs += [weight_shape(b) for b in g.branches]
    away_outs = range(1, len(outs))
    if sends:
        outs += face_shapes(1)
    scratch = [(16 * g.nz, 8, 128), (2, 256, 128), pltpu.SemaphoreType.DMA((len(g.branches),))]
    scratch += [weight_shape(b) for b in g.branches]
    for b in g.branches:
        scratch += [EXT[b]] * (5 if first else 3)
    kernel = functools.partial(cycle_kernel, g, own, first, final, sends)
    return call(kernel, outs, args + tuple(weights), scratch, away=len(weights), away_outs=away_outs)


def group_shapes(g):
    return [(g.fields, g.ns, 8, 128)] + [(g.nx, 8, 128)] * 2


def body(right_side, coefficients, first_guess):
    marks = []
    for axis in ("gx", "gy", "gz"):
        index = lax.axis_index(axis)
        marks += [index > 0, index < lax.axis_size(axis) - 1]
    m = jnp.stack(marks).astype(F32)

    sends = call(faces_kernel, face_shapes(2), (coefficients, first_guess), masked=False)
    faces = exchange_faces(sends)
    s1, xlo1, xhi1, s0, xlo0, xhi0, ylo, yhi, c = call(
        functools.partial(fields_kernel, (EARLY, LATE)),
        group_shapes(EARLY) + group_shapes(LATE) + [(OWN.no, 8, 128)] * 2 + [(1, ALL.ns, 8, 128)],
        (m, coefficients, first_guess, right_side) + faces,
        [(3, 512, 128)],
    )
    x1 = both("gx", xlo1, xhi1)
    y = both("gy", ylo, yhi)
    *x1, xlo0, xhi0 = lax.optimization_barrier((*x1, xlo0, xhi0))
    x1 = tuple(x1)
    x0 = both("gx", xlo0, xhi0)
    corner1, _ = corners_exchange(EARLY, m, *x1)
    arrays1 = (s1,) + x1 + y + corner1
    z1, _ = lanes_exchange(EARLY, OWN, m, arrays1)
    corner0, mark = corners_exchange(LATE, m, *x0, after=z1)
    arrays0 = (s0,) + x0 + y + corner0
    partial, weights1, weights2 = cycle(EARLY, OWN, True, False, False, (m,) + arrays1 + z1)
    z0, _ = lanes_exchange(LATE, OWN, m, arrays0, after=(partial,))
    out = cycle(LATE, OWN, True, True, True, (m,) + arrays0 + z0 + (first_guess, partial))
    field, weights0, sends = out[0], out[1], out[2:]

    ufaces = exchange_faces(sends)
    r, xlo, xhi, ylo, yhi = call(
        functools.partial(residual_kernel, ALL),
        group_shapes(ALL) + [(ALL.no, 8, 128)] * 2,
        (m, coefficients, field, right_side, c) + faces + ufaces,
        [(3, 512, 128)],
    )
    x = both("gx", xlo, xhi)
    y = both("gy", ylo, yhi)
    corner, _ = corners_exchange(ALL, m, *x, after=y)
    arrays = (r,) + x + y + corner
    z, _ = lanes_exchange(ALL, ALL, m, arrays)
    (field,) = cycle(ALL, ALL, False, True, False, (m,) + arrays + z + (field,), (weights0, weights1, weights2))
    return field


def solution(mesh):
    in_specs = (P("gx", "gy", "gz"), P(None, "gx", "gy", "gz"), P("gx", "gy", "gz"))
    out_specs = P("gx", "gy", "gz")
    return jax.shard_map(body, mesh=mesh, in_specs=in_specs, out_specs=out_specs, check_vma=False)
```

```python
import functools

import jax
import jax.numpy as jnp
from jax import lax
from jax.experimental import pallas as pl
from jax.experimental.pallas import tpu as pltpu
from jax.sharding import PartitionSpec as P

CYCLES = 2
SWEEPS = 8
relaxation = 0.8
blending = 0.4

PLANES = (8, 16, 16)
HALO = (8, 7, 7)
WIDE = (24, 30, 30)
ROWT = (2, 1, 2)
LANET = (2, 2, 1)
EXT = tuple((WIDE[b], LANET[b] + 1, 8 * (ROWT[b] + 2), 128) for b in range(3))
UNROLL = 4
F32 = jnp.float32
VMEM_LIMIT = 60 * 1024 * 1024
HIGHEST = lax.Precision.HIGHEST


class Layout:
    def __init__(self, branches, fields, joint=False):
        self.branches, self.fields = branches, fields
        self.s, self.z, self.x, self.own, self.corner = {}, {}, {}, {}, {}
        ns = nz = nx = no = nc = 0
        for b in branches:
            self.s[b], self.z[b] = ns, nz
            ns += ROWT[b] * LANET[b] * PLANES[b]
            nz += (ROWT[b] + 2) * WIDE[b]
        for f in range(fields):
            for b in branches:
                self.x[f, b], self.own[f, b], self.corner[f, b] = nx, no, nc
                nx += ROWT[b] * LANET[b] * depth(f, b)
                no += LANET[b] * PLANES[b]
                nc += LANET[b] * 2 * depth(f, b)
        if joint:
            self.own = {key: nc + at for key, at in self.own.items()}
            nc += no
        self.joint, self.ns, self.nx, self.no, self.nc, self.items = joint, ns, nx, no, nc, nz
        self.nz = (nz + 15) // 16


def depth(field, b):
    return HALO[b] - (field in (1, 3, 4))


ALL = Layout((0, 1, 2), 1)
EARLY = Layout((1, 2), 5)
LATE = Layout((0,), 5, joint=True)


def lane_of(shape):
    return lax.broadcasted_iota(jnp.int32, shape, len(shape) - 1)


def row_of(shape):
    return lax.broadcasted_iota(jnp.int32, shape, len(shape) - 2)


def pack_rows(load):
    groups = []
    for g in range(4):
        acc = jnp.zeros((8, 256), F32)
        for j in range(4):
            value, turn = load(4 * g + j)
            turn = (turn + 2 * j) % 8
            value = pltpu.roll(value, turn, 0) if turn else value
            acc = jnp.where(row_of((8, 256)) // 2 == j, value, acc)
        groups.append(acc)
    return groups


def pack_lanes(load):
    acc = jnp.zeros((16, 128), F32)
    for j in range(16):
        value, turn = load(j)
        turn = (turn + 8 * j) % 128
        value = pltpu.roll(value, turn, 1) if turn else value
        acc = jnp.where(lane_of((16, 128)) // 8 == j, value, acc)
    return acc


def send_faces(at, row_field, lane_field, yl, yh, zl, zh):
    for g, value in enumerate(pack_rows(lambda x: (row_field(x)[0:8, :], 0))):
        yl[at, g] = value
    for g, value in enumerate(pack_rows(lambda x: (row_field(x)[8:16, :], 2))):
        yh[at, g] = value
    zl[at] = pack_lanes(lambda x: (lane_field(x)[:, 0:128], 0))
    zh[at] = pack_lanes(lambda x: (lane_field(x)[:, 128:256], 8))


def faces_kernel(k, u, xl, xh, yl, yh, zl, zh):
    xl[0:1] = u[0:1]
    xl[1:3] = k[0, 0:2]
    xh[0:1] = u[15:16]
    xh[1:3] = k[0, 14:16]
    send_faces(0, lambda x: u[x], lambda x: u[x], yl, yh, zl, zh)
    send_faces(1, lambda x: k[1, x], lambda x: k[2, x], yl, yh, zl, zh)


def halo_rows(value, at, yl, yh, m):
    high, low = [], []
    for x in range(16):
        g, j = divmod(x, 4)
        high.append(pltpu.roll(yh[at, g], (8 - 2 * j) % 8, 0) if j else yh[at, g])
        turn = (6 - 2 * j) % 8
        low.append(pltpu.roll(yl[at, g], turn, 0) if turn else yl[at, g])
    high = jnp.stack(high) * m[3]
    low = jnp.stack(low) * m[2]
    return jnp.concatenate([value, high, low], axis=1)


def halo_lanes(value, at, zl, zh, m):
    high = zh[at] * m[5]
    low = zl[at] * m[4]
    lane = lane_of((16, 128))
    tiles = []
    for x in range(16):
        a = pltpu.roll(high, (128 - 8 * x) % 128, 1) if x else high
        b = pltpu.roll(low, 120 - 8 * x, 1) if x < 15 else low
        tiles.append(jnp.where(lane < 8, a, jnp.where(lane >= 120, b, 0.0)))
    return jnp.concatenate([value, jnp.stack(tiles)], axis=2)


def up(value, axis, keep):
    return keep(pltpu.roll(value, value.shape[axis] - 1, axis))


def down(value, axis, keep):
    return keep(pltpu.roll(value, 1, axis))


def lane_means(value, lanes):
    planes, rows, width = value.shape
    source = lax.broadcasted_iota(jnp.int32, (width, lanes), 0)
    target = lax.broadcasted_iota(jnp.int32, (width, lanes), 1)
    pair = source // 2
    pair = jnp.where(source >= 320, pair + 64, pair)
    matrix = jnp.where(pair == target, jnp.float32(0.5), jnp.float32(0.0))
    out = jnp.dot(value.reshape(planes * rows, width), matrix, precision=HIGHEST, preferred_element_type=F32)
    return out.reshape(planes, rows, lanes)


def row_means(value, scratch):
    planes, rows, width = value.shape
    count = planes * rows
    parts = []
    for t in range(width // 128):
        scratch[t, 0:count] = value[:, :, 128 * t : 128 * t + 128].reshape(count, 128)
        even = scratch[t, pl.ds(0, count // 2, stride=2), :]
        odd = scratch[t, pl.ds(1, count // 2, stride=2), :]
        parts.append((0.5 * (even + odd)).reshape(planes, rows // 2, 128))
    return jnp.concatenate(parts, axis=2)


def plane_means(value):
    planes = value.shape[0]
    value = value.reshape((planes // 2, 2) + value.shape[1:])
    return 0.5 * (value[:, 0] + value[:, 1])


def residual_of(k, u, f, kfaces, ufaces, m):
    xl, xh, yl, yh, zl, zh = kfaces
    uxl, uxh, uyl, uyh, uzl, uzh = ufaces
    own, rows, lanes = (lambda v: v), (lambda v: v[:, 0:16]), (lambda v: v[:, :, 0:256])
    v = u[...]
    k0 = k[0]
    vx = jnp.concatenate([uxl[0:1] * m[0], v, uxh[0:1] * m[1]], axis=0)
    kx = jnp.concatenate([xl[2:3] * m[0], k0, xh[1:2] * m[1]], axis=0)
    total = k[3] * v
    total = total + 0.5 * (k0 + kx[2:18]) * (v - vx[2:18]) + 0.5 * (k0 + kx[0:16]) * (v - vx[0:16])
    vy = halo_rows(v, 0, uyl, uyh, m)
    k1 = k[1]
    ky = halo_rows(k1, 1, yl, yh, m)
    total = total + 0.5 * (k1 + up(ky, 1, rows)) * (v - up(vy, 1, rows))
    total = total + 0.5 * (k1 + down(ky, 1, rows)) * (v - down(vy, 1, rows))
    vz = halo_lanes(v, 0, uzl, uzh, m)
    k2 = k[2]
    kz = halo_lanes(k2, 1, zl, zh, m)
    total = total + 0.5 * (k2 + up(kz, 2, lanes)) * (v - up(vz, 2, lanes))
    total = total + 0.5 * (k2 + down(kz, 2, lanes)) * (v - down(vz, 2, lanes))
    return f[...] - total, ky, kz


def put(g, out, field, b, value):
    for yt in range(ROWT[b]):
        for lt in range(LANET[b]):
            at = g.s[b] + (yt * LANET[b] + lt) * PLANES[b]
            out[field, at : at + PLANES[b]] = value[:, 8 * yt : 8 * yt + 8, 128 * lt : 128 * lt + 128]


def put_sides(g, out, field, b, xlo, xhi):
    h, p = depth(field, b), PLANES[b]
    for t in range(ROWT[b] * LANET[b]):
        to, at = g.x[field, b] + t * h, g.s[b] + t * p
        xlo[to : to + h] = out[field, at : at + h]
        xhi[to : to + h] = out[field, at + p - h : at + p]


def put_own_rows(g, out, field, b, ylo, yhi):
    p = PLANES[b]
    for lt in range(LANET[b]):
        at, first = g.own[field, b] + lt * p, g.s[b] + lt * p
        last = first + (ROWT[b] - 1) * LANET[b] * p
        ylo[at : at + p] = out[field, first : first + p]
        yhi[at : at + p] = out[field, last : last + p]


def coarse_residuals(r, scratch):
    return plane_means(r), row_means(r, scratch), lane_means(r, 128)


def fields_kernel(groups, m, k, u, f, xl, xh, yl, yh, zl, zh, *outs):
    scratch = outs[-1]
    faces = (xl, xh, yl, yh, zl, zh)
    r, ky, kz = residual_of(k, u, f, faces, faces, m)
    kx = jnp.concatenate([xl[1:3] * m[0], k[0], xh[1:3] * m[1]], axis=0)
    coarse = [
        (plane_means(kx), plane_means(ky), plane_means(kz), plane_means(k[3])),
        (row_means(kx[1:19], scratch), row_means(ky, scratch), row_means(kz, scratch), row_means(k[3], scratch)),
        (lane_means(kx[1:19], 128), lane_means(ky, 128), lane_means(kz, 256), lane_means(k[3], 128)),
    ]
    residuals = coarse_residuals(r, scratch)
    ylo, yhi, kept = outs[3 * len(groups) : 3 * len(groups) + 3]
    for b in range(3):
        cx, cy, cz, s = coarse[b]
        p, nr, nl = PLANES[b], 8 * ROWT[b], 128 * LANET[b]
        scale = [0.5, 0.5, 0.5]
        scale[b] = 0.125
        rows, lanes = (lambda v: v[:, 0:nr]), (lambda v: v[:, :, 0:nl])
        w0l = scale[0] * (cx[1 : p + 1] + cx[0:p])
        w0h = scale[0] * (cx[1 : p + 1] + cx[2 : p + 2])
        w1l = scale[1] * (rows(cy) + down(cy, 1, rows))
        w1h = scale[1] * (rows(cy) + up(cy, 1, rows))
        w2l = scale[2] * (lanes(cz) + down(cz, 2, lanes))
        w2h = scale[2] * (lanes(cz) + up(cz, 2, lanes))
        c = relaxation / (s + w0l + w0h + w1l + w1h + w2l + w2h)
        for i, g in enumerate(groups):
            if b in g.branches:
                out, xlo, xhi = outs[3 * i : 3 * i + 3]
                for field, value in enumerate((c * residuals[b], c, w0l, w1l, w2l)):
                    put(g, out, field, b, value)
                    put_sides(g, out, field, b, xlo, xhi)
                    if not g.joint:
                        put_own_rows(g, out, field, b, ylo, yhi)
        put(ALL, kept, 0, b, c)


def residual_kernel(g, m, k, u, f, c, *refs):
    faces, ufaces, (out, xlo, xhi, ylo, yhi, scratch) = refs[:6], refs[6:12], refs[12:]
    r, _, _ = residual_of(k, u, f, faces, ufaces, m)
    values = coarse_residuals(r, scratch)
    for b in g.branches:
        put(g, out, 0, b, values[b])
    out[...] = out[...] * c[...]
    for b in g.branches:
        put_sides(g, out, 0, b, xlo, xhi)
        put_own_rows(g, out, 0, b, ylo, yhi)


def pieces(g, field, b, yt, lt, m, s, xl, xh, yol, yoh, ycl, ych):
    h, p, hf = HALO[b], PLANES[b], depth(field, b)
    if yt < ROWT[b]:
        t = yt * LANET[b] + lt
        at, first = g.x[field, b] + t * hf, g.s[b] + t * p
        yield h - hf, hf, xl[at : at + hf] * m[0]
        yield h, p, s[field, first : first + p]
        yield h + p, hf, xh[at : at + hf] * m[1]
        return
    inner, outer, mask = (yoh, ych, m[3]) if yt == ROWT[b] else (yol, ycl, m[2])
    at, first = g.corner[field, b] + lt * 2 * hf, g.own[field, b] + lt * p
    yield h - hf, hf, outer[at : at + hf] * mask
    yield h, p, inner[first : first + p] * mask
    yield h + p, hf, outer[at + hf : at + 2 * hf] * mask


def corners_kernel(g, m, xl, xh, s, *rest):
    ylo, yhi = rest[-2:]
    for field in range(g.fields):
        for b in g.branches:
            if g.joint:
                put_own_rows(g, s, field, b, ylo, yhi)
            h = depth(field, b)
            for lt in range(LANET[b]):
                to = g.corner[field, b] + lt * 2 * h
                at = g.x[field, b] + lt * h
                last = at + (ROWT[b] - 1) * LANET[b] * h
                ylo[to : to + h] = xl[at : at + h] * m[0]
                ylo[to + h : to + 2 * h] = xh[at : at + h] * m[1]
                yhi[to : to + h] = xl[last : last + h] * m[0]
                yhi[to + h : to + 2 * h] = xh[last : last + h] * m[1]


def lanes_kernel(g, m, *rest):
    arrays = rest[:7]
    zlo, zhi, low, high = rest[-4:]
    nz = g.nz
    lane = lane_of((nz, 8, 128))
    if g.items < 16 * nz:
        low[g.items :] = jnp.zeros((16 * nz - g.items, 8, 128), F32)
        high[g.items :] = jnp.zeros((16 * nz - g.items, 8, 128), F32)
    for field in range(g.fields):
        for b in g.branches:
            for yt in range(ROWT[b] + 2):
                at = g.z[b] + yt * WIDE[b]
                for x, n, value in pieces(g, field, b, yt, 0, m, *arrays):
                    low[at + x : at + x + n] = value
                for x, n, value in pieces(g, field, b, yt, LANET[b] - 1, m, *arrays):
                    high[at + x : at + x + n] = value
        a = jnp.zeros((nz, 8, 128), F32)
        z = jnp.zeros((nz, 8, 128), F32)
        for j in range(16):
            v = low[nz * j : nz * j + nz]
            a = jnp.where(lane // 8 == j, pltpu.roll(v, 8 * j, 2) if j else v, a)
            v = high[nz * j : nz * j + nz]
            z = jnp.where(lane // 8 == j, pltpu.roll(v, 8 * j + 8, 2) if j < 15 else v, z)
        zlo[field] = a
        zhi[field] = z


def assemble(g, field, m, arrays, zl, zh, halo, ext):
    nz = g.nz
    lane = lane_of((nz, 8, 128))
    high = zh[field] * m[5]
    low = zl[field] * m[4]
    for j in range(16):
        a = pltpu.roll(high, 128 - 8 * j, 2) if j else high
        b = pltpu.roll(low, 120 - 8 * j, 2) if j < 15 else low
        halo[nz * j : nz * j + nz] = jnp.where(lane < 8, a, jnp.where(lane >= 120, b, 0.0))
    for b in g.branches:
        out = ext[b][field]
        for yt in range(ROWT[b] + 2):
            for lt in range(LANET[b]):
                for x, n, value in pieces(g, field, b, yt, lt, m, *arrays):
                    out[x : x + n, lt, 8 * yt : 8 * yt + 8, :] = value
            at = g.z[b] + yt * WIDE[b]
            out[:, LANET[b], 8 * yt : 8 * yt + 8, :] = halo[at : at + WIDE[b]]


def lane_shifted(tiles, lane):
    n = len(tiles)
    below = [pltpu.roll(v, 1, 1) for v in tiles]
    above = [pltpu.roll(v, 127, 1) for v in tiles]
    below = [jnp.where(lane == 0, below[t - 1], below[t]) for t in range(n)]
    above = [jnp.where(lane == 127, above[(t + 1) % n], above[t]) for t in range(n)]
    return below, above


def scaled_weights(b, ext, weights):
    wide, lanes, rows, _ = EXT[b]
    lane = lane_of((rows, 128))
    _, c_ref, w0_ref, w1_ref, w2_ref = ext

    def plane(x):
        w2 = [w2_ref[x, t] for t in range(lanes)]
        _, above = lane_shifted(w2, lane)
        outs = []
        for t in range(lanes):
            c, w1 = c_ref[x, t], w1_ref[x, t]
            sides = (w0_ref[x, t], w0_ref[x + 1, t], w1, pltpu.roll(w1, rows - 1, 0), w2[t], above[t])
            outs.append([c * v for v in sides])
        return outs

    def step(i, carry):
        outs = [plane(1 + 2 * i + j) for j in range(2)]
        for j, tiles in enumerate(outs):
            for t, values in enumerate(tiles):
                for side, value in enumerate(values):
                    weights[side, 1 + 2 * i + j, t] = value
        return carry

    lax.fori_loop(0, (wide - 2) // 2, step, 0)
    for x in (0, wide - 1):
        weights[:, x] = jnp.zeros((6, lanes, rows, 128), F32)


def sweeps(b, bias, slots, weights):
    wide, lanes, rows, _ = EXT[b]
    lane = lane_of((rows, 128))

    def plane(x, source):
        tiles = [source[x, t] for t in range(lanes)]
        below, above = lane_shifted(tiles, lane)
        outs = []
        for t, e in enumerate(tiles):
            total = bias[x, t] + (1.0 - relaxation) * e
            total = total + (weights[0, x, t] * source[x - 1, t] + weights[1, x, t] * source[x + 1, t])
            total = total + (weights[2, x, t] * pltpu.roll(e, 1, 0) + weights[3, x, t] * pltpu.roll(e, rows - 1, 0))
            total = total + (weights[4, x, t] * below[t] + weights[5, x, t] * above[t])
            outs.append(total)
        return outs

    source = bias
    for sweep in range(1, SWEEPS):
        target = slots[0] if source is not slots[0] else slots[1]

        def planes(start, count, source=source, target=target):
            outs = [plane(start + i, source) for i in range(count)]
            for i, tiles in enumerate(outs):
                for t, total in enumerate(tiles):
                    target[start + i, t] = total

        def step(i, carry, sweep=sweep, planes=planes):
            planes(sweep + i * UNROLL, UNROLL)
            return carry

        count = wide - 2 * sweep
        lax.fori_loop(0, count // UNROLL, step, 0)
        if count % UNROLL:
            planes(sweep + count - count % UNROLL, count % UNROLL)
        source = target
    return source


def correction_rows(e, joined):
    for x in range(16):
        for t in range(2):
            v = e[7 + x, t]
            even = 0.75 * v + 0.25 * pltpu.roll(v, 1, 0)
            odd = 0.75 * v + 0.25 * pltpu.roll(v, 23, 0)
            joined[t, pl.ds(16 * x, 8, stride=2), :] = even[0:8]
            joined[t, pl.ds(16 * x + 1, 8, stride=2), :] = odd[0:8]
    return jnp.concatenate([joined[0], joined[1]], axis=1).reshape(16, 16, 256)


def correction_lanes(e):
    source = lax.broadcasted_iota(jnp.int32, (256, 256), 0)
    target = lax.broadcasted_iota(jnp.int32, (256, 256), 1)
    near = target // 2
    far = (near + 2 * (target % 2) - 1 + 256) % 256
    matrix = jnp.where(source == near, 0.75, jnp.where(source == far, 0.25, 0.0)).astype(F32)
    values = jnp.concatenate([e[7:23, 0, 0:16, :], e[7:23, 1, 0:16, :]], axis=2).reshape(256, 256)
    out = jnp.dot(values, matrix, precision=HIGHEST, preferred_element_type=F32)
    return out.reshape(16, 16, 256)


def correction_planes(e):
    parts = []
    for t in range(2):
        middle, low, high = (e[i : i + 8, t, 0:16, :] for i in (8, 7, 9))
        even = 0.75 * middle + 0.25 * low
        odd = 0.75 * middle + 0.25 * high
        parts.append(jnp.stack([even, odd], axis=1).reshape(16, 16, 128))
    return jnp.concatenate(parts, axis=2)


def cycle_kernel(g, first, final, sends, *refs):
    refs = list(refs)

    def take(n):
        head = refs[:n]
        del refs[:n]
        return head

    n = len(g.branches)
    (m,) = take(1)
    arrays = take(7)
    zl, zh = take(2)
    u = take(1)[0] if final else None
    other = take(1)[0] if final and n < 3 else None
    stored = take(n) if not first else None
    (out,) = take(1)
    if first:
        stored = take(n)
    face_outs = take(6) if sends else None
    halo, joined, sem = take(3)
    weights = dict(zip(g.branches, take(n)))
    ext = {b: take(5 if first else 3) for b in g.branches}

    def copy(i, b):
        ends = (weights[b], stored[i]) if first else (stored[i], weights[b])
        return pltpu.make_async_copy(*ends, sem.at[i])

    if not first:
        for i, b in enumerate(g.branches):
            copy(i, b).start()
    for field in range(5 if first else 1):
        assemble(g, field, m, arrays, zl, zh, halo, ext)
    last = {}
    for i, b in enumerate(g.branches):
        if first:
            scaled_weights(b, ext[b], weights[b])
            copy(i, b).start()
        else:
            copy(i, b).wait()
        last[b] = sweeps(b, ext[b][0], ext[b][1:3], weights[b])
    total = other[...] if other is not None else None
    for b in g.branches:
        part = (correction_planes, lambda e: correction_rows(e, joined), correction_lanes)[b](last[b])
        total = part if total is None else total + part
    out[...] = u[...] + blending * total if final else total
    if sends:
        uxlo, uxhi, uylo, uyhi, uzlo, uzhi = face_outs
        uxlo[0:1] = out[0:1]
        uxhi[0:1] = out[15:16]
        send_faces(0, lambda x: out[x], lambda x: out[x], uylo, uyhi, uzlo, uzhi)
    if first:
        for i, b in enumerate(g.branches):
            copy(i, b).wait()


def ring(value, axis, step):
    n = lax.axis_size(axis)
    return lax.ppermute(value, axis, [(i, (i + step) % n) for i in range(n)])


def both(axis, to_low, to_high):
    return ring(to_high, axis, 1), ring(to_low, axis, -1)


def call(kernel, outs, args, scratch=(), masked=True, away=0, away_outs=()):
    vmem, anywhere = pl.BlockSpec(memory_space=pltpu.VMEM), pl.BlockSpec(memory_space=pl.ANY)
    specs = [vmem] * (len(args) - away) + [anywhere] * away
    if masked:
        specs[0] = pl.BlockSpec(memory_space=pltpu.SMEM)
    return pl.pallas_call(
        kernel,
        out_shape=[jax.ShapeDtypeStruct(shape, F32) for shape in outs],
        in_specs=specs,
        out_specs=[anywhere if i in away_outs else vmem for i in range(len(outs))],
        scratch_shapes=[pltpu.VMEM(shape, F32) if isinstance(shape, tuple) else shape for shape in scratch],
        compiler_params=pltpu.CompilerParams(vmem_limit_bytes=VMEM_LIMIT),
    )(*args)


def face_shapes(fields):
    return [(2 * fields - 1, 16, 256)] * 2 + [(fields, 4, 8, 256)] * 2 + [(fields, 16, 128)] * 2


def exchange_faces(sends):
    xlo, xhi, ylo, yhi, zlo, zhi = sends
    return both("gx", xlo, xhi) + both("gy", ylo, yhi) + both("gz", zlo, zhi)


def corners_exchange(g, m, s, xl, xh, after=()):
    ylo, yhi = call(
        functools.partial(corners_kernel, g),
        [(g.nc, 8, 128)] * 2,
        (m, xl, xh, s) + tuple(after),
        away=len(after) + (not g.joint),
    )
    return both("gy", ylo, yhi), ylo


def lanes_exchange(g, m, arrays, after=()):
    zlo, zhi = call(
        functools.partial(lanes_kernel, g),
        [(g.fields, g.nz, 8, 128)] * 2,
        (m,) + arrays + tuple(after),
        [(16 * g.nz, 8, 128)] * 2,
        away=len(after),
    )
    return both("gz", zlo, zhi), zlo


def weight_shape(b):
    return (6,) + EXT[b]


def cycle(g, first, final, sends, args, weights=()):
    outs = [(16, 16, 256)]
    if first:
        outs += [weight_shape(b) for b in g.branches]
    away_outs = range(1, len(outs))
    if sends:
        outs += face_shapes(1)
    scratch = [(16 * g.nz, 8, 128), (2, 256, 128), pltpu.SemaphoreType.DMA((len(g.branches),))]
    scratch += [weight_shape(b) for b in g.branches]
    for b in g.branches:
        scratch += [EXT[b]] * (5 if first else 3)
    kernel = functools.partial(cycle_kernel, g, first, final, sends)
    return call(kernel, outs, args + tuple(weights), scratch, away=len(weights), away_outs=away_outs)


def group_shapes(g):
    return [(g.fields, g.ns, 8, 128)] + [(g.nx, 8, 128)] * 2


def body(right_side, coefficients, first_guess):
    marks = []
    for axis in ("gx", "gy", "gz"):
        index = lax.axis_index(axis)
        marks += [index > 0, index < lax.axis_size(axis) - 1]
    m = jnp.stack(marks).astype(F32)

    sends = call(faces_kernel, face_shapes(2), (coefficients, first_guess), masked=False)
    faces = exchange_faces(sends)
    s1, xlo1, xhi1, s0, xlo0, xhi0, ylo, yhi, c = call(
        functools.partial(fields_kernel, (EARLY, LATE)),
        group_shapes(EARLY) + group_shapes(LATE) + [(EARLY.no, 8, 128)] * 2 + [(1, ALL.ns, 8, 128)],
        (m, coefficients, first_guess, right_side) + faces,
        [(3, 512, 128)],
    )
    x1 = both("gx", xlo1, xhi1)
    y = both("gy", ylo, yhi)
    *x1, xlo0, xhi0 = lax.optimization_barrier((*x1, xlo0, xhi0))
    x1 = tuple(x1)
    x0 = both("gx", xlo0, xhi0)
    corner1, _ = corners_exchange(EARLY, m, s1, *x1)
    arrays1 = (s1,) + x1 + y + corner1
    z1, _ = lanes_exchange(EARLY, m, arrays1)
    corner0, mark = corners_exchange(LATE, m, s0, *x0, after=z1)
    arrays0 = (s0,) + x0 + corner0 + corner0
    partial, weights1, weights2 = cycle(EARLY, True, False, False, (m,) + arrays1 + z1)
    z0, _ = lanes_exchange(LATE, m, arrays0, after=(partial,))
    out = cycle(LATE, True, True, True, (m,) + arrays0 + z0 + (first_guess, partial))
    field, weights0, sends = out[0], out[1], out[2:]

    ufaces = exchange_faces(sends)
    r, xlo, xhi, ylo, yhi = call(
        functools.partial(residual_kernel, ALL),
        group_shapes(ALL) + [(ALL.no, 8, 128)] * 2,
        (m, coefficients, field, right_side, c) + faces + ufaces,
        [(3, 512, 128)],
    )
    x = both("gx", xlo, xhi)
    y = both("gy", ylo, yhi)
    corner, _ = corners_exchange(ALL, m, r, *x, after=y)
    arrays = (r,) + x + y + corner
    z, _ = lanes_exchange(ALL, m, arrays)
    (field,) = cycle(ALL, False, True, False, (m,) + arrays + z + (field,), (weights0, weights1, weights2))
    return field


def solution(mesh):
    in_specs = (P("gx", "gy", "gz"), P(None, "gx", "gy", "gz"), P("gx", "gy", "gz"))
    out_specs = P("gx", "gy", "gz")
    return jax.shard_map(body, mesh=mesh, in_specs=in_specs, out_specs=out_specs, check_vma=False)
```

```python
import functools

import jax
import jax.numpy as jnp
from jax import lax
from jax.experimental import pallas as pl
from jax.experimental.pallas import tpu as pltpu
from jax.sharding import PartitionSpec as P

CYCLES = 2
SWEEPS = 8
relaxation = 0.8
blending = 0.4

PLANES = (8, 16, 16)
HALO = (8, 7, 7)
WIDE = (24, 30, 30)
ROWT = (2, 1, 2)
LANET = (2, 2, 1)
EXT = tuple((WIDE[b], LANET[b] + 1, 8 * (ROWT[b] + 2), 128) for b in range(3))
UNROLL = 4
F32 = jnp.float32
SMALL, LARGE = 24 * 1024 * 1024, 44 * 1024 * 1024
HIGHEST = lax.Precision.HIGHEST


class Layout:
    def __init__(self, branches, fields, joint=False):
        self.branches, self.fields = branches, fields
        self.s, self.z, self.x, self.own, self.corner = {}, {}, {}, {}, {}
        ns = nz = nx = no = nc = 0
        for b in branches:
            self.s[b], self.z[b] = ns, nz
            ns += ROWT[b] * LANET[b] * PLANES[b]
            nz += (ROWT[b] + 2) * WIDE[b]
        for f in range(fields):
            for b in branches:
                self.x[f, b], self.own[f, b], self.corner[f, b] = nx, no, nc
                nx += ROWT[b] * LANET[b] * depth(f, b)
                no += LANET[b] * PLANES[b]
                nc += LANET[b] * 2 * depth(f, b)
        if joint:
            self.own = {key: nc + at for key, at in self.own.items()}
            nc += no
        self.joint, self.ns, self.nx, self.no, self.nc, self.items = joint, ns, nx, no, nc, nz
        self.nz = (nz + 15) // 16


def depth(field, b):
    return HALO[b] - (field in (1, 3, 4))


ALL = Layout((0, 1, 2), 1)
EARLY = Layout((1, 2), 5)
LATE = Layout((0,), 5, joint=True)


def lane_of(shape):
    return lax.broadcasted_iota(jnp.int32, shape, len(shape) - 1)


def row_of(shape):
    return lax.broadcasted_iota(jnp.int32, shape, len(shape) - 2)


def pack_rows(load):
    groups = []
    for g in range(4):
        acc = jnp.zeros((8, 256), F32)
        for j in range(4):
            value, turn = load(4 * g + j)
            turn = (turn + 2 * j) % 8
            value = pltpu.roll(value, turn, 0) if turn else value
            acc = jnp.where(row_of((8, 256)) // 2 == j, value, acc)
        groups.append(acc)
    return groups


def pack_lanes(load):
    acc = jnp.zeros((16, 128), F32)
    for j in range(16):
        value, turn = load(j)
        turn = (turn + 8 * j) % 128
        value = pltpu.roll(value, turn, 1) if turn else value
        acc = jnp.where(lane_of((16, 128)) // 8 == j, value, acc)
    return acc


def send_faces(at, row_field, lane_field, yl, yh, zl, zh):
    for g, value in enumerate(pack_rows(lambda x: (row_field(x)[0:8, :], 0))):
        yl[at, g] = value
    for g, value in enumerate(pack_rows(lambda x: (row_field(x)[8:16, :], 2))):
        yh[at, g] = value
    zl[at] = pack_lanes(lambda x: (lane_field(x)[:, 0:128], 0))
    zh[at] = pack_lanes(lambda x: (lane_field(x)[:, 128:256], 8))


def faces_kernel(k, u, xl, xh, yl, yh, zl, zh):
    xl[0:1] = u[0:1]
    xl[1:3] = k[0, 0:2]
    xh[0:1] = u[15:16]
    xh[1:3] = k[0, 14:16]
    send_faces(0, lambda x: u[x], lambda x: u[x], yl, yh, zl, zh)
    send_faces(1, lambda x: k[1, x], lambda x: k[2, x], yl, yh, zl, zh)


def halo_rows(value, at, yl, yh, m):
    high, low = [], []
    for x in range(16):
        g, j = divmod(x, 4)
        high.append(pltpu.roll(yh[at, g], (8 - 2 * j) % 8, 0) if j else yh[at, g])
        turn = (6 - 2 * j) % 8
        low.append(pltpu.roll(yl[at, g], turn, 0) if turn else yl[at, g])
    high = jnp.stack(high) * m[3]
    low = jnp.stack(low) * m[2]
    return jnp.concatenate([value, high, low], axis=1)


def halo_lanes(value, at, zl, zh, m):
    high = zh[at] * m[5]
    low = zl[at] * m[4]
    lane = lane_of((16, 128))
    tiles = []
    for x in range(16):
        a = pltpu.roll(high, (128 - 8 * x) % 128, 1) if x else high
        b = pltpu.roll(low, 120 - 8 * x, 1) if x < 15 else low
        tiles.append(jnp.where(lane < 8, a, jnp.where(lane >= 120, b, 0.0)))
    return jnp.concatenate([value, jnp.stack(tiles)], axis=2)


def up(value, axis, keep):
    return keep(pltpu.roll(value, value.shape[axis] - 1, axis))


def down(value, axis, keep):
    return keep(pltpu.roll(value, 1, axis))


def lane_means(value, lanes):
    planes, rows, width = value.shape
    source = lax.broadcasted_iota(jnp.int32, (width, lanes), 0)
    target = lax.broadcasted_iota(jnp.int32, (width, lanes), 1)
    pair = source // 2
    pair = jnp.where(source >= 320, pair + 64, pair)
    matrix = jnp.where(pair == target, jnp.float32(0.5), jnp.float32(0.0))
    out = jnp.dot(value.reshape(planes * rows, width), matrix, precision=HIGHEST, preferred_element_type=F32)
    return out.reshape(planes, rows, lanes)


def row_means(value, scratch):
    planes, rows, width = value.shape
    count = planes * rows
    parts = []
    for t in range(width // 128):
        scratch[t, 0:count] = value[:, :, 128 * t : 128 * t + 128].reshape(count, 128)
        even = scratch[t, pl.ds(0, count // 2, stride=2), :]
        odd = scratch[t, pl.ds(1, count // 2, stride=2), :]
        parts.append((0.5 * (even + odd)).reshape(planes, rows // 2, 128))
    return jnp.concatenate(parts, axis=2)


def plane_means(value):
    planes = value.shape[0]
    value = value.reshape((planes // 2, 2) + value.shape[1:])
    return 0.5 * (value[:, 0] + value[:, 1])


def residual_of(k, u, f, kfaces, ufaces, m):
    xl, xh, yl, yh, zl, zh = kfaces
    uxl, uxh, uyl, uyh, uzl, uzh = ufaces
    own, rows, lanes = (lambda v: v), (lambda v: v[:, 0:16]), (lambda v: v[:, :, 0:256])
    v = u[...]
    k0 = k[0]
    vx = jnp.concatenate([uxl[0:1] * m[0], v, uxh[0:1] * m[1]], axis=0)
    kx = jnp.concatenate([xl[2:3] * m[0], k0, xh[1:2] * m[1]], axis=0)
    total = k[3] * v
    total = total + 0.5 * (k0 + kx[2:18]) * (v - vx[2:18]) + 0.5 * (k0 + kx[0:16]) * (v - vx[0:16])
    vy = halo_rows(v, 0, uyl, uyh, m)
    k1 = k[1]
    ky = halo_rows(k1, 1, yl, yh, m)
    total = total + 0.5 * (k1 + up(ky, 1, rows)) * (v - up(vy, 1, rows))
    total = total + 0.5 * (k1 + down(ky, 1, rows)) * (v - down(vy, 1, rows))
    vz = halo_lanes(v, 0, uzl, uzh, m)
    k2 = k[2]
    kz = halo_lanes(k2, 1, zl, zh, m)
    total = total + 0.5 * (k2 + up(kz, 2, lanes)) * (v - up(vz, 2, lanes))
    total = total + 0.5 * (k2 + down(kz, 2, lanes)) * (v - down(vz, 2, lanes))
    return f[...] - total, ky, kz


def put(g, out, field, b, value):
    for yt in range(ROWT[b]):
        for lt in range(LANET[b]):
            at = g.s[b] + (yt * LANET[b] + lt) * PLANES[b]
            out[field, at : at + PLANES[b]] = value[:, 8 * yt : 8 * yt + 8, 128 * lt : 128 * lt + 128]


def put_sides(g, out, field, b, xlo, xhi):
    h, p = depth(field, b), PLANES[b]
    for t in range(ROWT[b] * LANET[b]):
        to, at = g.x[field, b] + t * h, g.s[b] + t * p
        xlo[to : to + h] = out[field, at : at + h]
        xhi[to : to + h] = out[field, at + p - h : at + p]


def put_own_rows(g, out, field, b, ylo, yhi):
    p = PLANES[b]
    for lt in range(LANET[b]):
        at, first = g.own[field, b] + lt * p, g.s[b] + lt * p
        last = first + (ROWT[b] - 1) * LANET[b] * p
        ylo[at : at + p] = out[field, first : first + p]
        yhi[at : at + p] = out[field, last : last + p]


def coarse_residuals(r, scratch):
    return plane_means(r), row_means(r, scratch), lane_means(r, 128)


def fields_kernel(groups, m, k, u, f, xl, xh, yl, yh, zl, zh, *outs):
    scratch = outs[-1]
    faces = (xl, xh, yl, yh, zl, zh)
    r, ky, kz = residual_of(k, u, f, faces, faces, m)
    kx = jnp.concatenate([xl[1:3] * m[0], k[0], xh[1:3] * m[1]], axis=0)
    coarse = [
        (plane_means(kx), plane_means(ky), plane_means(kz), plane_means(k[3])),
        (row_means(kx[1:19], scratch), row_means(ky, scratch), row_means(kz, scratch), row_means(k[3], scratch)),
        (lane_means(kx[1:19], 128), lane_means(ky, 128), lane_means(kz, 256), lane_means(k[3], 128)),
    ]
    residuals = coarse_residuals(r, scratch)
    ylo, yhi, kept = outs[3 * len(groups) : 3 * len(groups) + 3]
    for b in range(3):
        cx, cy, cz, s = coarse[b]
        p, nr, nl = PLANES[b], 8 * ROWT[b], 128 * LANET[b]
        scale = [0.5, 0.5, 0.5]
        scale[b] = 0.125
        rows, lanes = (lambda v: v[:, 0:nr]), (lambda v: v[:, :, 0:nl])
        w0l = scale[0] * (cx[1 : p + 1] + cx[0:p])
        w0h = scale[0] * (cx[1 : p + 1] + cx[2 : p + 2])
        w1l = scale[1] * (rows(cy) + down(cy, 1, rows))
        w1h = scale[1] * (rows(cy) + up(cy, 1, rows))
        w2l = scale[2] * (lanes(cz) + down(cz, 2, lanes))
        w2h = scale[2] * (lanes(cz) + up(cz, 2, lanes))
        c = relaxation / (s + w0l + w0h + w1l + w1h + w2l + w2h)
        for i, g in enumerate(groups):
            if b in g.branches:
                out, xlo, xhi = outs[3 * i : 3 * i + 3]
                for field, value in enumerate((c * residuals[b], c, w0l, w1l, w2l)):
                    put(g, out, field, b, value)
                    put_sides(g, out, field, b, xlo, xhi)
                    if not g.joint:
                        put_own_rows(g, out, field, b, ylo, yhi)
        put(ALL, kept, 0, b, c)


def residual_kernel(g, m, k, u, f, c, *refs):
    faces, ufaces, (out, xlo, xhi, ylo, yhi, scratch) = refs[:6], refs[6:12], refs[12:]
    r, _, _ = residual_of(k, u, f, faces, ufaces, m)
    values = coarse_residuals(r, scratch)
    for b in g.branches:
        put(g, out, 0, b, values[b])
    out[...] = out[...] * c[...]
    for b in g.branches:
        put_sides(g, out, 0, b, xlo, xhi)
        put_own_rows(g, out, 0, b, ylo, yhi)


def pieces(g, field, b, yt, lt, m, s, xl, xh, yol, yoh, ycl, ych):
    h, p, hf = HALO[b], PLANES[b], depth(field, b)
    if yt < ROWT[b]:
        t = yt * LANET[b] + lt
        at, first = g.x[field, b] + t * hf, g.s[b] + t * p
        yield h - hf, hf, xl[at : at + hf] * m[0]
        yield h, p, s[field, first : first + p]
        yield h + p, hf, xh[at : at + hf] * m[1]
        return
    inner, outer, mask = (yoh, ych, m[3]) if yt == ROWT[b] else (yol, ycl, m[2])
    at, first = g.corner[field, b] + lt * 2 * hf, g.own[field, b] + lt * p
    yield h - hf, hf, outer[at : at + hf] * mask
    yield h, p, inner[first : first + p] * mask
    yield h + p, hf, outer[at + hf : at + 2 * hf] * mask


def corners_kernel(g, m, xl, xh, s, *rest):
    ylo, yhi = rest[-2:]
    for field in range(g.fields):
        for b in g.branches:
            if g.joint:
                put_own_rows(g, s, field, b, ylo, yhi)
            h = depth(field, b)
            for lt in range(LANET[b]):
                to = g.corner[field, b] + lt * 2 * h
                at = g.x[field, b] + lt * h
                last = at + (ROWT[b] - 1) * LANET[b] * h
                ylo[to : to + h] = xl[at : at + h] * m[0]
                ylo[to + h : to + 2 * h] = xh[at : at + h] * m[1]
                yhi[to : to + h] = xl[last : last + h] * m[0]
                yhi[to + h : to + 2 * h] = xh[last : last + h] * m[1]


def lanes_kernel(g, m, *rest):
    arrays = rest[:7]
    zlo, zhi, low, high = rest[-4:]
    nz = g.nz
    lane = lane_of((nz, 8, 128))
    if g.items < 16 * nz:
        low[g.items :] = jnp.zeros((16 * nz - g.items, 8, 128), F32)
        high[g.items :] = jnp.zeros((16 * nz - g.items, 8, 128), F32)
    for field in range(g.fields):
        for b in g.branches:
            for yt in range(ROWT[b] + 2):
                at = g.z[b] + yt * WIDE[b]
                for x, n, value in pieces(g, field, b, yt, 0, m, *arrays):
                    low[at + x : at + x + n] = value
                for x, n, value in pieces(g, field, b, yt, LANET[b] - 1, m, *arrays):
                    high[at + x : at + x + n] = value
        a = jnp.zeros((nz, 8, 128), F32)
        z = jnp.zeros((nz, 8, 128), F32)
        for j in range(16):
            v = low[nz * j : nz * j + nz]
            a = jnp.where(lane // 8 == j, pltpu.roll(v, 8 * j, 2) if j else v, a)
            v = high[nz * j : nz * j + nz]
            z = jnp.where(lane // 8 == j, pltpu.roll(v, 8 * j + 8, 2) if j < 15 else v, z)
        zlo[field] = a
        zhi[field] = z


def assemble(g, field, m, arrays, zl, zh, halo, ext):
    nz = g.nz
    lane = lane_of((nz, 8, 128))
    high = zh[field] * m[5]
    low = zl[field] * m[4]
    for j in range(16):
        a = pltpu.roll(high, 128 - 8 * j, 2) if j else high
        b = pltpu.roll(low, 120 - 8 * j, 2) if j < 15 else low
        halo[nz * j : nz * j + nz] = jnp.where(lane < 8, a, jnp.where(lane >= 120, b, 0.0))
    for b in g.branches:
        out = ext[b][field]
        for yt in range(ROWT[b] + 2):
            for lt in range(LANET[b]):
                for x, n, value in pieces(g, field, b, yt, lt, m, *arrays):
                    out[x : x + n, lt, 8 * yt : 8 * yt + 8, :] = value
            at = g.z[b] + yt * WIDE[b]
            out[:, LANET[b], 8 * yt : 8 * yt + 8, :] = halo[at : at + WIDE[b]]


def lane_shifted(tiles, lane):
    n = len(tiles)
    below = [pltpu.roll(v, 1, 1) for v in tiles]
    above = [pltpu.roll(v, 127, 1) for v in tiles]
    below = [jnp.where(lane == 0, below[t - 1], below[t]) for t in range(n)]
    above = [jnp.where(lane == 127, above[(t + 1) % n], above[t]) for t in range(n)]
    return below, above


def scaled_weights(b, ext, weights):
    wide, lanes, rows, _ = EXT[b]
    lane = lane_of((rows, 128))
    _, c_ref, w0_ref, w1_ref, w2_ref = ext

    def plane(x):
        w2 = [w2_ref[x, t] for t in range(lanes)]
        _, above = lane_shifted(w2, lane)
        outs = []
        for t in range(lanes):
            c, w1 = c_ref[x, t], w1_ref[x, t]
            sides = (w0_ref[x, t], w0_ref[x + 1, t], w1, pltpu.roll(w1, rows - 1, 0), w2[t], above[t])
            outs.append([c * v for v in sides])
        return outs

    def step(i, carry):
        outs = [plane(1 + 2 * i + j) for j in range(2)]
        for j, tiles in enumerate(outs):
            for t, values in enumerate(tiles):
                for side, value in enumerate(values):
                    weights[side, 1 + 2 * i + j, t] = value
        return carry

    lax.fori_loop(0, (wide - 2) // 2, step, 0)
    for x in (0, wide - 1):
        weights[:, x] = jnp.zeros((6, lanes, rows, 128), F32)


def sweeps(b, bias, slots, weights):
    wide, lanes, rows, _ = EXT[b]
    lane = lane_of((rows, 128))

    def plane(x, source):
        tiles = [source[x, t] for t in range(lanes)]
        below, above = lane_shifted(tiles, lane)
        outs = []
        for t, e in enumerate(tiles):
            total = bias[x, t] + (1.0 - relaxation) * e
            total = total + (weights[0, x, t] * source[x - 1, t] + weights[1, x, t] * source[x + 1, t])
            total = total + (weights[2, x, t] * pltpu.roll(e, 1, 0) + weights[3, x, t] * pltpu.roll(e, rows - 1, 0))
            total = total + (weights[4, x, t] * below[t] + weights[5, x, t] * above[t])
            outs.append(total)
        return outs

    source = bias
    for sweep in range(1, SWEEPS):
        target = slots[0] if source is not slots[0] else slots[1]

        def planes(start, count, source=source, target=target):
            outs = [plane(start + i, source) for i in range(count)]
            for i, tiles in enumerate(outs):
                for t, total in enumerate(tiles):
                    target[start + i, t] = total

        def step(i, carry, sweep=sweep, planes=planes):
            planes(sweep + i * UNROLL, UNROLL)
            return carry

        count = wide - 2 * sweep
        lax.fori_loop(0, count // UNROLL, step, 0)
        if count % UNROLL:
            planes(sweep + count - count % UNROLL, count % UNROLL)
        source = target
    return source


def correction_rows(e, joined):
    for x in range(16):
        for t in range(2):
            v = e[7 + x, t]
            even = 0.75 * v + 0.25 * pltpu.roll(v, 1, 0)
            odd = 0.75 * v + 0.25 * pltpu.roll(v, 23, 0)
            joined[t, pl.ds(16 * x, 8, stride=2), :] = even[0:8]
            joined[t, pl.ds(16 * x + 1, 8, stride=2), :] = odd[0:8]
    return jnp.concatenate([joined[0], joined[1]], axis=1).reshape(16, 16, 256)


def correction_lanes(e):
    source = lax.broadcasted_iota(jnp.int32, (256, 256), 0)
    target = lax.broadcasted_iota(jnp.int32, (256, 256), 1)
    near = target // 2
    far = (near + 2 * (target % 2) - 1 + 256) % 256
    matrix = jnp.where(source == near, 0.75, jnp.where(source == far, 0.25, 0.0)).astype(F32)
    values = jnp.concatenate([e[7:23, 0, 0:16, :], e[7:23, 1, 0:16, :]], axis=2).reshape(256, 256)
    out = jnp.dot(values, matrix, precision=HIGHEST, preferred_element_type=F32)
    return out.reshape(16, 16, 256)


def correction_planes(e):
    parts = []
    for t in range(2):
        middle, low, high = (e[i : i + 8, t, 0:16, :] for i in (8, 7, 9))
        even = 0.75 * middle + 0.25 * low
        odd = 0.75 * middle + 0.25 * high
        parts.append(jnp.stack([even, odd], axis=1).reshape(16, 16, 128))
    return jnp.concatenate(parts, axis=2)


def cycle_kernel(g, first, final, sends, *refs):
    refs = list(refs)

    def take(n):
        head = refs[:n]
        del refs[:n]
        return head

    n = len(g.branches)
    (m,) = take(1)
    arrays = take(7)
    zl, zh = take(2)
    u = take(1)[0] if final else None
    other = take(1)[0] if final and n < 3 else None
    stored = take(n) if not first else None
    (out,) = take(1)
    if first:
        stored = take(n)
    face_outs = take(6) if sends else None
    halo, joined, sem = take(3)
    weights = dict(zip(g.branches, take(n)))
    ext = {b: take(5 if first else 3) for b in g.branches}

    def copy(i, b):
        ends = (weights[b], stored[i]) if first else (stored[i], weights[b])
        return pltpu.make_async_copy(*ends, sem.at[i])

    if not first:
        for i, b in enumerate(g.branches):
            copy(i, b).start()
    for field in range(5 if first else 1):
        assemble(g, field, m, arrays, zl, zh, halo, ext)
    last = {}
    for i, b in enumerate(g.branches):
        if first:
            scaled_weights(b, ext[b], weights[b])
            copy(i, b).start()
        else:
            copy(i, b).wait()
        last[b] = sweeps(b, ext[b][0], ext[b][1:3], weights[b])
    total = other[...] if other is not None else None
    for b in g.branches:
        part = (correction_planes, lambda e: correction_rows(e, joined), correction_lanes)[b](last[b])
        total = part if total is None else total + part
    out[...] = u[...] + blending * total if final else total
    if sends:
        uxlo, uxhi, uylo, uyhi, uzlo, uzhi = face_outs
        uxlo[0:1] = out[0:1]
        uxhi[0:1] = out[15:16]
        send_faces(0, lambda x: out[x], lambda x: out[x], uylo, uyhi, uzlo, uzhi)
    if first:
        for i, b in enumerate(g.branches):
            copy(i, b).wait()


def ring(value, axis, step):
    n = lax.axis_size(axis)
    return lax.ppermute(value, axis, [(i, (i + step) % n) for i in range(n)])


def both(axis, to_low, to_high):
    return ring(to_high, axis, 1), ring(to_low, axis, -1)


def call(kernel, outs, args, scratch=(), masked=True, away=0, away_outs=(), limit=SMALL):
    vmem, anywhere = pl.BlockSpec(memory_space=pltpu.VMEM), pl.BlockSpec(memory_space=pl.ANY)
    specs = [vmem] * (len(args) - away) + [anywhere] * away
    if masked:
        specs[0] = pl.BlockSpec(memory_space=pltpu.SMEM)
    return pl.pallas_call(
        kernel,
        out_shape=[jax.ShapeDtypeStruct(shape, F32) for shape in outs],
        in_specs=specs,
        out_specs=[anywhere if i in away_outs else vmem for i in range(len(outs))],
        scratch_shapes=[pltpu.VMEM(shape, F32) if isinstance(shape, tuple) else shape for shape in scratch],
        compiler_params=pltpu.CompilerParams(vmem_limit_bytes=limit),
    )(*args)


def face_shapes(fields):
    return [(2 * fields - 1, 16, 256)] * 2 + [(fields, 4, 8, 256)] * 2 + [(fields, 16, 128)] * 2


def exchange_faces(sends):
    xlo, xhi, ylo, yhi, zlo, zhi = sends
    return both("gx", xlo, xhi) + both("gy", ylo, yhi) + both("gz", zlo, zhi)


def corners_exchange(g, m, s, xl, xh, after=()):
    ylo, yhi = call(
        functools.partial(corners_kernel, g),
        [(g.nc, 8, 128)] * 2,
        (m, xl, xh, s) + tuple(after),
        away=len(after) + (not g.joint),
    )
    return both("gy", ylo, yhi), ylo


def lanes_exchange(g, m, arrays, after=()):
    zlo, zhi = call(
        functools.partial(lanes_kernel, g),
        [(g.fields, g.nz, 8, 128)] * 2,
        (m,) + arrays + tuple(after),
        [(16 * g.nz, 8, 128)] * 2,
        away=len(after),
    )
    return both("gz", zlo, zhi), zlo


def weight_shape(b):
    return (6,) + EXT[b]


def cycle(g, first, final, sends, args, weights=()):
    outs = [(16, 16, 256)]
    if first:
        outs += [weight_shape(b) for b in g.branches]
    away_outs = range(1, len(outs))
    if sends:
        outs += face_shapes(1)
    scratch = [(16 * g.nz, 8, 128), (2, 256, 128), pltpu.SemaphoreType.DMA((len(g.branches),))]
    scratch += [weight_shape(b) for b in g.branches]
    for b in g.branches:
        scratch += [EXT[b]] * (5 if first else 3)
    kernel = functools.partial(cycle_kernel, g, first, final, sends)
    return call(kernel, outs, args + tuple(weights), scratch, away=len(weights), away_outs=away_outs, limit=LARGE)


def group_shapes(g):
    return [(g.fields, g.ns, 8, 128)] + [(g.nx, 8, 128)] * 2


def body(right_side, coefficients, first_guess):
    marks = []
    for axis in ("gx", "gy", "gz"):
        index = lax.axis_index(axis)
        marks += [index > 0, index < lax.axis_size(axis) - 1]
    m = jnp.stack(marks).astype(F32)

    sends = call(faces_kernel, face_shapes(2), (coefficients, first_guess), masked=False)
    faces = exchange_faces(sends)
    s1, xlo1, xhi1, s0, xlo0, xhi0, ylo, yhi, c = call(
        functools.partial(fields_kernel, (EARLY, LATE)),
        group_shapes(EARLY) + group_shapes(LATE) + [(EARLY.no, 8, 128)] * 2 + [(1, ALL.ns, 8, 128)],
        (m, coefficients, first_guess, right_side) + faces,
        [(3, 512, 128)],
    )
    x1 = both("gx", xlo1, xhi1)
    y = both("gy", ylo, yhi)
    *x1, xlo0, xhi0 = lax.optimization_barrier((*x1, xlo0, xhi0))
    x1 = tuple(x1)
    x0 = both("gx", xlo0, xhi0)
    corner1, _ = corners_exchange(EARLY, m, s1, *x1)
    arrays1 = (s1,) + x1 + y + corner1
    z1, _ = lanes_exchange(EARLY, m, arrays1)
    corner0, mark = corners_exchange(LATE, m, s0, *x0, after=z1)
    arrays0 = (s0,) + x0 + corner0 + corner0
    partial, weights1, weights2 = cycle(EARLY, True, False, False, (m,) + arrays1 + z1)
    z0, _ = lanes_exchange(LATE, m, arrays0, after=(partial,))
    out = cycle(LATE, True, True, True, (m,) + arrays0 + z0 + (first_guess, partial))
    field, weights0, sends = out[0], out[1], out[2:]

    ufaces = exchange_faces(sends)
    r, xlo, xhi, ylo, yhi = call(
        functools.partial(residual_kernel, ALL),
        group_shapes(ALL) + [(ALL.no, 8, 128)] * 2,
        (m, coefficients, field, right_side, c) + faces + ufaces,
        [(3, 512, 128)],
    )
    x = both("gx", xlo, xhi)
    y = both("gy", ylo, yhi)
    corner, _ = corners_exchange(ALL, m, r, *x, after=y)
    arrays = (r,) + x + y + corner
    z, _ = lanes_exchange(ALL, m, arrays)
    (field,) = cycle(ALL, False, True, False, (m,) + arrays + z + (field,), (weights0, weights1, weights2))
    return field


def solution(mesh):
    in_specs = (P("gx", "gy", "gz"), P(None, "gx", "gy", "gz"), P("gx", "gy", "gz"))
    out_specs = P("gx", "gy", "gz")
    return jax.shard_map(body, mesh=mesh, in_specs=in_specs, out_specs=out_specs, check_vma=False)
```

```python
import functools

import jax
import jax.numpy as jnp
from jax import lax
from jax.experimental import pallas as pl
from jax.experimental.pallas import tpu as pltpu
from jax.sharding import PartitionSpec as P

CYCLES = 2
SWEEPS = 8
relaxation = 0.8
blending = 0.4

PLANES = (8, 16, 16)
HALO = (8, 7, 7)
WIDE = (24, 30, 30)
ROWT = (2, 1, 2)
LANET = (2, 2, 1)
EXT = tuple((WIDE[b], LANET[b] + 1, 8 * (ROWT[b] + 2), 128) for b in range(3))
UNROLL = 4
F32 = jnp.float32
SMALL, LARGE = 24 * 1024 * 1024, 44 * 1024 * 1024
HIGHEST = lax.Precision.HIGHEST


class Layout:
    def __init__(self, branches, fields, joint=False):
        self.branches, self.fields = branches, fields
        self.s, self.z, self.x, self.own, self.corner = {}, {}, {}, {}, {}
        ns = nz = nx = no = nc = 0
        for b in branches:
            self.s[b], self.z[b] = ns, nz
            ns += ROWT[b] * LANET[b] * PLANES[b]
            nz += (ROWT[b] + 2) * WIDE[b]
        for f in range(fields):
            for b in branches:
                self.x[f, b], self.own[f, b], self.corner[f, b] = nx, no, nc
                nx += ROWT[b] * LANET[b] * depth(f, b)
                no += LANET[b] * PLANES[b]
                nc += LANET[b] * 2 * depth(f, b)
        if joint:
            self.own = {key: nc + at for key, at in self.own.items()}
            nc += no
        self.joint, self.ns, self.nx, self.no, self.nc, self.items = joint, ns, nx, no, nc, nz
        self.nz = (nz + 15) // 16


def depth(field, b):
    return HALO[b] - (field in (1, 3, 4))


ALL = Layout((0, 1, 2), 1)
EARLY = Layout((1, 2), 5)
LATE = Layout((0,), 5, joint=True)


def lane_of(shape):
    return lax.broadcasted_iota(jnp.int32, shape, len(shape) - 1)


def row_of(shape):
    return lax.broadcasted_iota(jnp.int32, shape, len(shape) - 2)


def pack_rows(load):
    groups = []
    for g in range(4):
        acc = jnp.zeros((8, 256), F32)
        for j in range(4):
            value, turn = load(4 * g + j)
            turn = (turn + 2 * j) % 8
            value = pltpu.roll(value, turn, 0) if turn else value
            acc = jnp.where(row_of((8, 256)) // 2 == j, value, acc)
        groups.append(acc)
    return groups


def pack_lanes(load):
    acc = jnp.zeros((16, 128), F32)
    for j in range(16):
        value, turn = load(j)
        turn = (turn + 8 * j) % 128
        value = pltpu.roll(value, turn, 1) if turn else value
        acc = jnp.where(lane_of((16, 128)) // 8 == j, value, acc)
    return acc


def send_faces(at, row_field, lane_field, yl, yh, zl, zh):
    for g, value in enumerate(pack_rows(lambda x: (row_field(x)[0:8, :], 0))):
        yl[at, g] = value
    for g, value in enumerate(pack_rows(lambda x: (row_field(x)[8:16, :], 2))):
        yh[at, g] = value
    zl[at] = pack_lanes(lambda x: (lane_field(x)[:, 0:128], 0))
    zh[at] = pack_lanes(lambda x: (lane_field(x)[:, 128:256], 8))


def faces_kernel(k, u, xl, xh, yl, yh, zl, zh, kout, uout):
    kout[...] = k[...]
    uout[...] = u[...]
    xl[0:1] = u[0:1]
    xl[1:3] = k[0, 0:2]
    xh[0:1] = u[15:16]
    xh[1:3] = k[0, 14:16]
    send_faces(0, lambda x: u[x], lambda x: u[x], yl, yh, zl, zh)
    send_faces(1, lambda x: k[1, x], lambda x: k[2, x], yl, yh, zl, zh)


def halo_rows(value, at, yl, yh, m):
    high, low = [], []
    for x in range(16):
        g, j = divmod(x, 4)
        high.append(pltpu.roll(yh[at, g], (8 - 2 * j) % 8, 0) if j else yh[at, g])
        turn = (6 - 2 * j) % 8
        low.append(pltpu.roll(yl[at, g], turn, 0) if turn else yl[at, g])
    high = jnp.stack(high) * m[3]
    low = jnp.stack(low) * m[2]
    return jnp.concatenate([value, high, low], axis=1)


def halo_lanes(value, at, zl, zh, m):
    high = zh[at] * m[5]
    low = zl[at] * m[4]
    lane = lane_of((16, 128))
    tiles = []
    for x in range(16):
        a = pltpu.roll(high, (128 - 8 * x) % 128, 1) if x else high
        b = pltpu.roll(low, 120 - 8 * x, 1) if x < 15 else low
        tiles.append(jnp.where(lane < 8, a, jnp.where(lane >= 120, b, 0.0)))
    return jnp.concatenate([value, jnp.stack(tiles)], axis=2)


def up(value, axis, keep):
    return keep(pltpu.roll(value, value.shape[axis] - 1, axis))


def down(value, axis, keep):
    return keep(pltpu.roll(value, 1, axis))


def lane_means(value, lanes):
    planes, rows, width = value.shape
    source = lax.broadcasted_iota(jnp.int32, (width, lanes), 0)
    target = lax.broadcasted_iota(jnp.int32, (width, lanes), 1)
    pair = source // 2
    pair = jnp.where(source >= 320, pair + 64, pair)
    matrix = jnp.where(pair == target, jnp.float32(0.5), jnp.float32(0.0))
    out = jnp.dot(value.reshape(planes * rows, width), matrix, precision=HIGHEST, preferred_element_type=F32)
    return out.reshape(planes, rows, lanes)


def row_means(value, scratch):
    planes, rows, width = value.shape
    count = planes * rows
    parts = []
    for t in range(width // 128):
        scratch[t, 0:count] = value[:, :, 128 * t : 128 * t + 128].reshape(count, 128)
        even = scratch[t, pl.ds(0, count // 2, stride=2), :]
        odd = scratch[t, pl.ds(1, count // 2, stride=2), :]
        parts.append((0.5 * (even + odd)).reshape(planes, rows // 2, 128))
    return jnp.concatenate(parts, axis=2)


def plane_means(value):
    planes = value.shape[0]
    value = value.reshape((planes // 2, 2) + value.shape[1:])
    return 0.5 * (value[:, 0] + value[:, 1])


def residual_of(k, u, f, kfaces, ufaces, m):
    xl, xh, yl, yh, zl, zh = kfaces
    uxl, uxh, uyl, uyh, uzl, uzh = ufaces
    own, rows, lanes = (lambda v: v), (lambda v: v[:, 0:16]), (lambda v: v[:, :, 0:256])
    v = u[...]
    k0 = k[0]
    vx = jnp.concatenate([uxl[0:1] * m[0], v, uxh[0:1] * m[1]], axis=0)
    kx = jnp.concatenate([xl[2:3] * m[0], k0, xh[1:2] * m[1]], axis=0)
    total = k[3] * v
    total = total + 0.5 * (k0 + kx[2:18]) * (v - vx[2:18]) + 0.5 * (k0 + kx[0:16]) * (v - vx[0:16])
    vy = halo_rows(v, 0, uyl, uyh, m)
    k1 = k[1]
    ky = halo_rows(k1, 1, yl, yh, m)
    total = total + 0.5 * (k1 + up(ky, 1, rows)) * (v - up(vy, 1, rows))
    total = total + 0.5 * (k1 + down(ky, 1, rows)) * (v - down(vy, 1, rows))
    vz = halo_lanes(v, 0, uzl, uzh, m)
    k2 = k[2]
    kz = halo_lanes(k2, 1, zl, zh, m)
    total = total + 0.5 * (k2 + up(kz, 2, lanes)) * (v - up(vz, 2, lanes))
    total = total + 0.5 * (k2 + down(kz, 2, lanes)) * (v - down(vz, 2, lanes))
    return f[...] - total, ky, kz


def put(g, out, field, b, value):
    for yt in range(ROWT[b]):
        for lt in range(LANET[b]):
            at = g.s[b] + (yt * LANET[b] + lt) * PLANES[b]
            out[field, at : at + PLANES[b]] = value[:, 8 * yt : 8 * yt + 8, 128 * lt : 128 * lt + 128]


def put_sides(g, out, field, b, xlo, xhi):
    h, p = depth(field, b), PLANES[b]
    for t in range(ROWT[b] * LANET[b]):
        to, at = g.x[field, b] + t * h, g.s[b] + t * p
        xlo[to : to + h] = out[field, at : at + h]
        xhi[to : to + h] = out[field, at + p - h : at + p]


def put_own_rows(g, out, field, b, ylo, yhi):
    p = PLANES[b]
    for lt in range(LANET[b]):
        at, first = g.own[field, b] + lt * p, g.s[b] + lt * p
        last = first + (ROWT[b] - 1) * LANET[b] * p
        ylo[at : at + p] = out[field, first : first + p]
        yhi[at : at + p] = out[field, last : last + p]


def coarse_residuals(r, scratch):
    return plane_means(r), row_means(r, scratch), lane_means(r, 128)


def fields_kernel(groups, m, k, u, f, xl, xh, yl, yh, zl, zh, *outs):
    scratch = outs[-1]
    faces = (xl, xh, yl, yh, zl, zh)
    r, ky, kz = residual_of(k, u, f, faces, faces, m)
    kx = jnp.concatenate([xl[1:3] * m[0], k[0], xh[1:3] * m[1]], axis=0)
    coarse = [
        (plane_means(kx), plane_means(ky), plane_means(kz), plane_means(k[3])),
        (row_means(kx[1:19], scratch), row_means(ky, scratch), row_means(kz, scratch), row_means(k[3], scratch)),
        (lane_means(kx[1:19], 128), lane_means(ky, 128), lane_means(kz, 256), lane_means(k[3], 128)),
    ]
    residuals = coarse_residuals(r, scratch)
    ylo, yhi, kept = outs[3 * len(groups) : 3 * len(groups) + 3]
    for b in range(3):
        cx, cy, cz, s = coarse[b]
        p, nr, nl = PLANES[b], 8 * ROWT[b], 128 * LANET[b]
        scale = [0.5, 0.5, 0.5]
        scale[b] = 0.125
        rows, lanes = (lambda v: v[:, 0:nr]), (lambda v: v[:, :, 0:nl])
        w0l = scale[0] * (cx[1 : p + 1] + cx[0:p])
        w0h = scale[0] * (cx[1 : p + 1] + cx[2 : p + 2])
        w1l = scale[1] * (rows(cy) + down(cy, 1, rows))
        w1h = scale[1] * (rows(cy) + up(cy, 1, rows))
        w2l = scale[2] * (lanes(cz) + down(cz, 2, lanes))
        w2h = scale[2] * (lanes(cz) + up(cz, 2, lanes))
        c = relaxation / (s + w0l + w0h + w1l + w1h + w2l + w2h)
        for i, g in enumerate(groups):
            if b in g.branches:
                out, xlo, xhi = outs[3 * i : 3 * i + 3]
                for field, value in enumerate((c * residuals[b], c, w0l, w1l, w2l)):
                    put(g, out, field, b, value)
                    put_sides(g, out, field, b, xlo, xhi)
                    if not g.joint:
                        put_own_rows(g, out, field, b, ylo, yhi)
        put(ALL, kept, 0, b, c)


def residual_kernel(g, m, k, u, f, c, *refs):
    faces, ufaces, (out, xlo, xhi, ylo, yhi, scratch) = refs[:6], refs[6:12], refs[12:]
    r, _, _ = residual_of(k, u, f, faces, ufaces, m)
    values = coarse_residuals(r, scratch)
    for b in g.branches:
        put(g, out, 0, b, values[b])
    out[...] = out[...] * c[...]
    for b in g.branches:
        put_sides(g, out, 0, b, xlo, xhi)
        put_own_rows(g, out, 0, b, ylo, yhi)


def pieces(g, field, b, yt, lt, m, s, xl, xh, yol, yoh, ycl, ych):
    h, p, hf = HALO[b], PLANES[b], depth(field, b)
    if yt < ROWT[b]:
        t = yt * LANET[b] + lt
        at, first = g.x[field, b] + t * hf, g.s[b] + t * p
        yield h - hf, hf, xl[at : at + hf] * m[0]
        yield h, p, s[field, first : first + p]
        yield h + p, hf, xh[at : at + hf] * m[1]
        return
    inner, outer, mask = (yoh, ych, m[3]) if yt == ROWT[b] else (yol, ycl, m[2])
    at, first = g.corner[field, b] + lt * 2 * hf, g.own[field, b] + lt * p
    yield h - hf, hf, outer[at : at + hf] * mask
    yield h, p, inner[first : first + p] * mask
    yield h + p, hf, outer[at + hf : at + 2 * hf] * mask


def corners_kernel(g, m, xl, xh, s, *rest):
    ylo, yhi = rest[-2:]
    for field in range(g.fields):
        for b in g.branches:
            if g.joint:
                put_own_rows(g, s, field, b, ylo, yhi)
            h = depth(field, b)
            for lt in range(LANET[b]):
                to = g.corner[field, b] + lt * 2 * h
                at = g.x[field, b] + lt * h
                last = at + (ROWT[b] - 1) * LANET[b] * h
                ylo[to : to + h] = xl[at : at + h] * m[0]
                ylo[to + h : to + 2 * h] = xh[at : at + h] * m[1]
                yhi[to : to + h] = xl[last : last + h] * m[0]
                yhi[to + h : to + 2 * h] = xh[last : last + h] * m[1]


def lanes_kernel(g, m, *rest):
    arrays = rest[:7]
    zlo, zhi, low, high = rest[-4:]
    nz = g.nz
    lane = lane_of((nz, 8, 128))
    if g.items < 16 * nz:
        low[g.items :] = jnp.zeros((16 * nz - g.items, 8, 128), F32)
        high[g.items :] = jnp.zeros((16 * nz - g.items, 8, 128), F32)
    for field in range(g.fields):
        for b in g.branches:
            for yt in range(ROWT[b] + 2):
                at = g.z[b] + yt * WIDE[b]
                for x, n, value in pieces(g, field, b, yt, 0, m, *arrays):
                    low[at + x : at + x + n] = value
                for x, n, value in pieces(g, field, b, yt, LANET[b] - 1, m, *arrays):
                    high[at + x : at + x + n] = value
        a = jnp.zeros((nz, 8, 128), F32)
        z = jnp.zeros((nz, 8, 128), F32)
        for j in range(16):
            v = low[nz * j : nz * j + nz]
            a = jnp.where(lane // 8 == j, pltpu.roll(v, 8 * j, 2) if j else v, a)
            v = high[nz * j : nz * j + nz]
            z = jnp.where(lane // 8 == j, pltpu.roll(v, 8 * j + 8, 2) if j < 15 else v, z)
        zlo[field] = a
        zhi[field] = z


def assemble(g, field, m, arrays, zl, zh, halo, ext):
    nz = g.nz
    lane = lane_of((nz, 8, 128))
    high = zh[field] * m[5]
    low = zl[field] * m[4]
    for j in range(16):
        a = pltpu.roll(high, 128 - 8 * j, 2) if j else high
        b = pltpu.roll(low, 120 - 8 * j, 2) if j < 15 else low
        halo[nz * j : nz * j + nz] = jnp.where(lane < 8, a, jnp.where(lane >= 120, b, 0.0))
    for b in g.branches:
        out = ext[b][field]
        for yt in range(ROWT[b] + 2):
            for lt in range(LANET[b]):
                for x, n, value in pieces(g, field, b, yt, lt, m, *arrays):
                    out[x : x + n, lt, 8 * yt : 8 * yt + 8, :] = value
            at = g.z[b] + yt * WIDE[b]
            out[:, LANET[b], 8 * yt : 8 * yt + 8, :] = halo[at : at + WIDE[b]]


def lane_shifted(tiles, lane):
    n = len(tiles)
    below = [pltpu.roll(v, 1, 1) for v in tiles]
    above = [pltpu.roll(v, 127, 1) for v in tiles]
    below = [jnp.where(lane == 0, below[t - 1], below[t]) for t in range(n)]
    above = [jnp.where(lane == 127, above[(t + 1) % n], above[t]) for t in range(n)]
    return below, above


def scaled_weights(b, ext, weights):
    wide, lanes, rows, _ = EXT[b]
    lane = lane_of((rows, 128))
    _, c_ref, w0_ref, w1_ref, w2_ref = ext

    def plane(x):
        w2 = [w2_ref[x, t] for t in range(lanes)]
        _, above = lane_shifted(w2, lane)
        outs = []
        for t in range(lanes):
            c, w1 = c_ref[x, t], w1_ref[x, t]
            sides = (w0_ref[x, t], w0_ref[x + 1, t], w1, pltpu.roll(w1, rows - 1, 0), w2[t], above[t])
            outs.append([c * v for v in sides])
        return outs

    def step(i, carry):
        outs = [plane(1 + 2 * i + j) for j in range(2)]
        for j, tiles in enumerate(outs):
            for t, values in enumerate(tiles):
                for side, value in enumerate(values):
                    weights[side, 1 + 2 * i + j, t] = value
        return carry

    lax.fori_loop(0, (wide - 2) // 2, step, 0)
    for x in (0, wide - 1):
        weights[:, x] = jnp.zeros((6, lanes, rows, 128), F32)


def sweeps(b, bias, slots, weights):
    wide, lanes, rows, _ = EXT[b]
    lane = lane_of((rows, 128))

    def plane(x, source, nr, nt):
        tiles = [source[x, t] for t in range(lanes)]
        below, above = lane_shifted(tiles, lane)
        outs = []
        for t in range(nt):
            e = tiles[t]
            rolled = pltpu.roll(e, 1, 0)[0:nr], pltpu.roll(e, rows - 1, 0)[0:nr]
            w = [weights[side, x, t, 0:nr, :] for side in range(6)]
            total = bias[x, t, 0:nr, :] + (1.0 - relaxation) * e[0:nr]
            total = total + (w[0] * source[x - 1, t, 0:nr, :] + w[1] * source[x + 1, t, 0:nr, :])
            total = total + (w[2] * rolled[0] + w[3] * rolled[1])
            total = total + (w[4] * below[t][0:nr] + w[5] * above[t][0:nr])
            outs.append(total)
        return outs

    source = bias
    for sweep in range(1, SWEEPS):
        target = slots[0] if source is not slots[0] else slots[1]
        nr, nt = (rows, lanes) if sweep < SWEEPS - 1 else (rows if b == 1 else rows - 16, 2)

        def planes(start, count, source=source, target=target, nr=nr, nt=nt):
            outs = [plane(start + i, source, nr, nt) for i in range(count)]
            for i, tiles in enumerate(outs):
                for t, total in enumerate(tiles):
                    target[start + i, t, 0:nr, :] = total

        def step(i, carry, sweep=sweep, planes=planes):
            planes(sweep + i * UNROLL, UNROLL)
            return carry

        count = wide - 2 * sweep
        lax.fori_loop(0, count // UNROLL, step, 0)
        if count % UNROLL:
            planes(sweep + count - count % UNROLL, count % UNROLL)
        source = target
    return source


def correction_rows(e, joined):
    for x in range(16):
        for t in range(2):
            v = e[7 + x, t]
            even = 0.75 * v + 0.25 * pltpu.roll(v, 1, 0)
            odd = 0.75 * v + 0.25 * pltpu.roll(v, 23, 0)
            joined[t, pl.ds(16 * x, 8, stride=2), :] = even[0:8]
            joined[t, pl.ds(16 * x + 1, 8, stride=2), :] = odd[0:8]
    return jnp.concatenate([joined[0], joined[1]], axis=1).reshape(16, 16, 256)


def correction_lanes(e):
    source = lax.broadcasted_iota(jnp.int32, (256, 256), 0)
    target = lax.broadcasted_iota(jnp.int32, (256, 256), 1)
    near = target // 2
    far = (near + 2 * (target % 2) - 1 + 256) % 256
    matrix = jnp.where(source == near, 0.75, jnp.where(source == far, 0.25, 0.0)).astype(F32)
    values = jnp.concatenate([e[7:23, 0, 0:16, :], e[7:23, 1, 0:16, :]], axis=2).reshape(256, 256)
    out = jnp.dot(values, matrix, precision=HIGHEST, preferred_element_type=F32)
    return out.reshape(16, 16, 256)


def correction_planes(e):
    parts = []
    for t in range(2):
        middle, low, high = (e[i : i + 8, t, 0:16, :] for i in (8, 7, 9))
        even = 0.75 * middle + 0.25 * low
        odd = 0.75 * middle + 0.25 * high
        parts.append(jnp.stack([even, odd], axis=1).reshape(16, 16, 128))
    return jnp.concatenate(parts, axis=2)


def cycle_kernel(g, first, final, sends, *refs):
    refs = list(refs)

    def take(n):
        head = refs[:n]
        del refs[:n]
        return head

    n = len(g.branches)
    (m,) = take(1)
    arrays = take(7)
    zl, zh = take(2)
    u = take(1)[0] if final else None
    other = take(1)[0] if final and n < 3 else None
    stored = take(n) if not first else None
    (out,) = take(1)
    if first:
        stored = take(n)
    face_outs = take(6) if sends else None
    halo, joined, sem = take(3)
    weights = dict(zip(g.branches, take(n)))
    ext = {b: take(5 if first else 3) for b in g.branches}

    def copy(i, b):
        ends = (weights[b], stored[i]) if first else (stored[i], weights[b])
        return pltpu.make_async_copy(*ends, sem.at[i])

    if not first:
        for i, b in enumerate(g.branches):
            copy(i, b).start()
    for field in range(5 if first else 1):
        assemble(g, field, m, arrays, zl, zh, halo, ext)
    last = {}
    for i, b in enumerate(g.branches):
        if first:
            scaled_weights(b, ext[b], weights[b])
            copy(i, b).start()
        else:
            copy(i, b).wait()
        last[b] = sweeps(b, ext[b][0], ext[b][1:3], weights[b])
    total = other[...] if other is not None else None
    for b in g.branches:
        part = (correction_planes, lambda e: correction_rows(e, joined), correction_lanes)[b](last[b])
        total = part if total is None else total + part
    out[...] = u[...] + blending * total if final else total
    if sends:
        uxlo, uxhi, uylo, uyhi, uzlo, uzhi = face_outs
        uxlo[0:1] = out[0:1]
        uxhi[0:1] = out[15:16]
        send_faces(0, lambda x: out[x], lambda x: out[x], uylo, uyhi, uzlo, uzhi)
    if first:
        for i, b in enumerate(g.branches):
            copy(i, b).wait()


def ring(value, axis, step):
    n = lax.axis_size(axis)
    return lax.ppermute(value, axis, [(i, (i + step) % n) for i in range(n)])


def both(axis, to_low, to_high):
    return ring(to_high, axis, 1), ring(to_low, axis, -1)


def call(kernel, outs, args, scratch=(), masked=True, away=0, away_outs=(), limit=SMALL):
    vmem, anywhere = pl.BlockSpec(memory_space=pltpu.VMEM), pl.BlockSpec(memory_space=pl.ANY)
    specs = [vmem] * (len(args) - away) + [anywhere] * away
    if masked:
        specs[0] = pl.BlockSpec(memory_space=pltpu.SMEM)
    return pl.pallas_call(
        kernel,
        out_shape=[jax.ShapeDtypeStruct(shape, F32) for shape in outs],
        in_specs=specs,
        out_specs=[anywhere if i in away_outs else vmem for i in range(len(outs))],
        scratch_shapes=[pltpu.VMEM(shape, F32) if isinstance(shape, tuple) else shape for shape in scratch],
        compiler_params=pltpu.CompilerParams(vmem_limit_bytes=limit),
    )(*args)


def face_shapes(fields):
    return [(2 * fields - 1, 16, 256)] * 2 + [(fields, 4, 8, 256)] * 2 + [(fields, 16, 128)] * 2


def exchange_faces(sends):
    xlo, xhi, ylo, yhi, zlo, zhi = sends
    return both("gx", xlo, xhi) + both("gy", ylo, yhi) + both("gz", zlo, zhi)


def corners_exchange(g, m, s, xl, xh, after=()):
    ylo, yhi = call(
        functools.partial(corners_kernel, g),
        [(g.nc, 8, 128)] * 2,
        (m, xl, xh, s) + tuple(after),
        away=len(after) + (not g.joint),
    )
    return both("gy", ylo, yhi), ylo


def lanes_exchange(g, m, arrays, after=()):
    zlo, zhi = call(
        functools.partial(lanes_kernel, g),
        [(g.fields, g.nz, 8, 128)] * 2,
        (m,) + arrays + tuple(after),
        [(16 * g.nz, 8, 128)] * 2,
        away=len(after),
    )
    return both("gz", zlo, zhi), zlo


def weight_shape(b):
    return (6,) + EXT[b]


def cycle(g, first, final, sends, args, weights=()):
    outs = [(16, 16, 256)]
    if first:
        outs += [weight_shape(b) for b in g.branches]
    away_outs = range(1, len(outs))
    if sends:
        outs += face_shapes(1)
    scratch = [(16 * g.nz, 8, 128), (2, 256, 128), pltpu.SemaphoreType.DMA((len(g.branches),))]
    scratch += [weight_shape(b) for b in g.branches]
    for b in g.branches:
        scratch += [EXT[b]] * (5 if first else 3)
    kernel = functools.partial(cycle_kernel, g, first, final, sends)
    return call(kernel, outs, args + tuple(weights), scratch, away=len(weights), away_outs=away_outs, limit=LARGE)


def group_shapes(g):
    return [(g.fields, g.ns, 8, 128)] + [(g.nx, 8, 128)] * 2


def body(right_side, coefficients, first_guess):
    marks = []
    for axis in ("gx", "gy", "gz"):
        index = lax.axis_index(axis)
        marks += [index > 0, index < lax.axis_size(axis) - 1]
    m = jnp.stack(marks).astype(F32)

    *sends, coefficients, first_guess = call(
        faces_kernel,
        face_shapes(2) + [(4, 16, 16, 256), (16, 16, 256)],
        (coefficients, first_guess),
        masked=False,
    )
    faces = exchange_faces(sends)
    s1, xlo1, xhi1, s0, xlo0, xhi0, ylo, yhi, c = call(
        functools.partial(fields_kernel, (EARLY, LATE)),
        group_shapes(EARLY) + group_shapes(LATE) + [(EARLY.no, 8, 128)] * 2 + [(1, ALL.ns, 8, 128)],
        (m, coefficients, first_guess, right_side) + faces,
        [(3, 512, 128)],
    )
    x1 = both("gx", xlo1, xhi1)
    y = both("gy", ylo, yhi)
    *x1, xlo0, xhi0 = lax.optimization_barrier((*x1, xlo0, xhi0))
    x1 = tuple(x1)
    x0 = both("gx", xlo0, xhi0)
    corner1, _ = corners_exchange(EARLY, m, s1, *x1)
    arrays1 = (s1,) + x1 + y + corner1
    z1, _ = lanes_exchange(EARLY, m, arrays1)
    corner0, mark = corners_exchange(LATE, m, s0, *x0, after=z1)
    arrays0 = (s0,) + x0 + corner0 + corner0
    partial, weights1, weights2 = cycle(EARLY, True, False, False, (m,) + arrays1 + z1)
    z0, _ = lanes_exchange(LATE, m, arrays0, after=(partial,))
    out = cycle(LATE, True, True, True, (m,) + arrays0 + z0 + (first_guess, partial))
    field, weights0, sends = out[0], out[1], out[2:]

    ufaces = exchange_faces(sends)
    r, xlo, xhi, ylo, yhi = call(
        functools.partial(residual_kernel, ALL),
        group_shapes(ALL) + [(ALL.no, 8, 128)] * 2,
        (m, coefficients, field, right_side, c) + faces + ufaces,
        [(3, 512, 128)],
    )
    x = both("gx", xlo, xhi)
    y = both("gy", ylo, yhi)
    corner, _ = corners_exchange(ALL, m, r, *x, after=y)
    arrays = (r,) + x + y + corner
    z, _ = lanes_exchange(ALL, m, arrays)
    (field,) = cycle(ALL, False, True, False, (m,) + arrays + z + (field,), (weights0, weights1, weights2))
    return field


def solution(mesh):
    in_specs = (P("gx", "gy", "gz"), P(None, "gx", "gy", "gz"), P("gx", "gy", "gz"))
    out_specs = P("gx", "gy", "gz")
    return jax.shard_map(body, mesh=mesh, in_specs=in_specs, out_specs=out_specs, check_vma=False)
```
